128 devices in a mesh: dp: 16 (over z, y), ctx: 2 (over core), mp: 4 (over x).
Axes of the slice: x: 4, y: 4, z: 4, core: 2. Of those that a mesh axis runs over, the one named last changes fastest.
Arguments:
- tokens: bfloat16 [16, 1024, 1024], P('dp', 'ctx'), may hold values from -6 to 6
- attn_in: bfloat16 [2, 1024, 3, 1024], P(None, ('dp', 'ctx'), None, 'mp'), may hold values from -0.1875 to 0.1875
- attn_out: bfloat16 [2, 1024, 1024], P(None, ('dp', 'ctx'), 'mp'), may hold values from -0.5 to 0.5
- mlp_in: bfloat16 [2, 1024, 4096], P(None, ('dp', 'ctx'), 'mp'), may hold values from -0.1875 to 0.1875
- mlp_out: bfloat16 [2, 1024, 4096], P(None, ('dp', 'ctx'), 'mp'), may hold values from -0.09375 to 0.09375
- norm_gain: float32 [2, 2, 1024], replicated, may hold values from 0.25 to 1.75
- norm_shift: float32 [2, 2, 1024], replicated, may hold values from -3 to 3
- head_bias: float32 [2, 2, 1024], P(None, None, 'mp'), may hold values from -3 to 3
- unit_bias: float32 [2, 4096], P(None, 'mp'), may hold values from -3 to 3
- branch_bias: float32 [2, 2, 1024], replicated, may hold values from -3 to 3
- cotangent: bfloat16 [16, 1024, 1024], P('dp', 'ctx'), may hold values from -6 to 6
Outputs:
- mixed: bfloat16 [16, 1024, 1024], P('dp', 'ctx')
- token_grad: float32 [16, 1024, 1024], P('dp', 'ctx')
- attn_in_grad: float32 [2, 1024, 3, 1024], P(None, ('dp', 'ctx'), None, 'mp')
- attn_out_grad: float32 [2, 1024, 1024], P(None, ('dp', 'ctx'), 'mp')
- mlp_in_grad: float32 [2, 1024, 4096], P(None, ('dp', 'ctx'), 'mp')
- mlp_out_grad: float32 [2, 1024, 4096], P(None, ('dp', 'ctx'), 'mp')
- norm_gain_grad: float32 [2, 2, 1024], replicated
- norm_shift_grad: float32 [2, 2, 1024], replicated
- head_bias_grad: float32 [2, 2, 1024], P(None, None, 'mp')
- unit_bias_grad: float32 [2, 4096], P(None, 'mp')
- branch_bias_grad: float32 [2, 2, 1024], replicated
The draws below stay inside these ranges and needn't reach their ends.
All inputs are finite; a program needn't handle non-finite values.
Results may differ from the reference program's by a relative error of at most 0.025.
Values may be sent and summed in bfloat16 or wider, within the bound.
No kernel may reach another device: no remote copies, remote signals or barrier semaphores. Data moves between devices by JAX's collectives and lax.ppermute only.
A program may use at most 128 MiB of HBM per device.

```python
import jax
import jax.numpy as jnp
from jax import lax

D = 1024
HEADS = 16
HEAD_DIM = 64
FF = 4096
LAYERS = 2
SEQ_LEN = 1024
SEQS = 16


def strengthened(drawn, rng, source, target, blocks, factor):
    def block_of(position):
        return (jnp.arange(drawn.shape[position]) // (drawn.shape[position] // blocks)).reshape((-1,) + (1,) * (drawn.ndim - 1 - position))

    one_side = jax.random.permutation(rng, blocks)[block_of(target)]
    second = (block_of(target) + blocks // 2) % blocks
    return jnp.where((block_of(source) == one_side) | (block_of(source) == second), factor * drawn, drawn)


def steps_of(rng, dims, split, low, high):
    level, own = 1.0, jax.random.fold_in(rng, 6)
    for position, shards_of in split:
        heights = jnp.exp(jax.random.uniform(jax.random.fold_in(own, position), (shards_of,), jnp.float32, low / len(split), high / len(split)))
        level = level * jnp.repeat(heights, dims[position] // shards_of).reshape([-1 if axis == position else 1 for axis in range(len(dims))])
    return level


def noise(rng, shape, width, most, cuts=(), kind=jnp.bfloat16):
    loudness = steps_of(rng, shape, cuts, -0.22, 0.18) if cuts else 1.0
    values = jax.random.normal(rng, shape, jnp.float32) * width * loudness
    return jnp.minimum(jnp.maximum(values, -most), most).astype(kind)


def bell_draw_with(stream_key, dims, spread, most, shards, heavy, held_as=jnp.bfloat16):
    drawn = spread * jax.random.normal(stream_key, dims, jnp.float32)
    if shards:
        drawn = drawn * steps_of(stream_key, dims, shards, -0.22, 0.18)
    return jnp.clip(strengthened(drawn, jax.random.fold_in(stream_key, 3), *heavy), -most, most).astype(held_as)


def setup_inputs(seed: int = 0) -> dict:
    arg_keys = jax.random.split(jax.random.key(seed), 12)
    return {
        "tokens": noise(arg_keys[0], (SEQS, SEQ_LEN, D), 1.0, 6.0, ((0, 16), (1, 2))),
        "attn_in": noise(arg_keys[1], (LAYERS, D, 3, D), D ** -0.5, 0.1875, ((1, 32), (3, 4))),
        "attn_out": noise(arg_keys[2], (LAYERS, D, D), (D // 8) ** -0.5, 0.5, ((1, 32), (2, 4))),
        "mlp_in": noise(arg_keys[3], (LAYERS, D, FF), D ** -0.5, 0.1875, ((1, 32), (2, 4))),
        "mlp_out": noise(arg_keys[4], (LAYERS, D, FF), FF ** -0.5, 0.09375, ((1, 32), (2, 4))),
        "norm_gain": jnp.clip(1.0 + 0.15 * jax.random.normal(arg_keys[5], (LAYERS, 2, D), jnp.float32), 0.25, 1.75),
        "norm_shift": noise(arg_keys[6], (LAYERS, 2, D), 0.2, 3.0, (), jnp.float32),
        "head_bias": noise(arg_keys[7], (LAYERS, 2, D), 0.2, 3.0, ((2, 4),), jnp.float32),
        "unit_bias": noise(arg_keys[8], (LAYERS, FF), 0.2, 3.0, ((1, 4),), jnp.float32),
        "branch_bias": noise(arg_keys[9], (LAYERS, 2, D), 0.2, 3.0, (), jnp.float32),
        "cotangent": bell_draw_with(arg_keys[10], (SEQS, SEQ_LEN, D), 1.0, 6.0, ((0, 16), (1, 2)), (0, 2, 16, 2.0)),
    }


EPS = 1e-05
HIGH = lax.Precision.HIGHEST

@jax.custom_vjp
def low(v):
    return lax.optimization_barrier(v.astype(jnp.bfloat16)).astype(jnp.float32)

@jax.custom_vjp
def low_back(v):
    return v

def low_keep(v):
    return (low(v), None)

def low_pass(kept, grad):
    return (grad,)

def back_keep(v):
    return (v, None)

def back_low(kept, grad):
    return (low(grad),)
low.defvjp(low_keep, low_pass)
low_back.defvjp(back_keep, back_low)

def product(left, right):
    return jnp.dot(left, right, precision=HIGH, preferred_element_type=jnp.float32)

def normalize(value, gain, shift):
    mean = lax.optimization_barrier(jnp.mean(value, axis=-1, keepdims=True))
    centred = value - mean
    variance = lax.optimization_barrier(jnp.mean(centred * centred, axis=-1, keepdims=True))
    return centred * lax.rsqrt(variance + EPS) * gain + shift

def attention(query, keys, values):
    length = query.shape[0]
    query = query.reshape(length, HEADS, HEAD_DIM).transpose(1, 0, 2)
    keys = keys.reshape(length, HEADS, HEAD_DIM).transpose(1, 0, 2)
    values = values.reshape(length, HEADS, HEAD_DIM).transpose(1, 0, 2)
    rows_at = lax.broadcasted_iota(jnp.int32, (length, length), 0)
    cols_at = lax.broadcasted_iota(jnp.int32, (length, length), 1)
    causal = cols_at <= rows_at
    scale = HEAD_DIM ** (-0.5)

    def one_head(triple):
        head_q, head_k, head_v = triple
        scores = low_back(product(head_q, head_k.T) * scale)
        scores = jnp.where(causal, scores, -1e+30)
        weights = jax.nn.softmax(scores, axis=-1)
        return product(low(weights), head_v)
    outputs = lax.map(jax.checkpoint(one_head), (query, keys, values))
    return outputs.transpose(1, 0, 2).reshape(length, HEADS * HEAD_DIM)

def forward(sequence, params):
    attn_in, attn_out, mlp_in, mlp_out, norm_gain, norm_shift, head_bias, unit_bias, branch_bias = params
    state = sequence
    for layer in range(LAYERS):
        normed = low(normalize(state, norm_gain[layer, 0], norm_shift[layer, 0]))
        projected = product(normed, attn_in[layer].reshape(D, 3 * D))
        query = low(low_back(projected[:, :D]) + head_bias[layer, 0])
        keys = low(low_back(projected[:, D:2 * D]))
        values = low(low_back(projected[:, 2 * D:]) + head_bias[layer, 1])
        heads_out = low(low_back(attention(query, keys, values)))
        state = state + low_back(product(heads_out, attn_out[layer].T)) + branch_bias[layer, 0]
        second = low(normalize(state, norm_gain[layer, 1], norm_shift[layer, 1]))
        hidden = low_back(product(second, mlp_in[layer])) + unit_bias[layer]
        active = low(jax.nn.gelu(hidden, approximate=True))
        state = state + low_back(product(active, mlp_out[layer].T)) + branch_bias[layer, 1]
    return state

def reference(tokens, attn_in, attn_out, mlp_in, mlp_out, norm_gain, norm_shift, head_bias, unit_bias, branch_bias, cotangent):
    params = tuple((item.astype(jnp.float32) for item in (attn_in, attn_out, mlp_in, mlp_out, norm_gain, norm_shift, head_bias, unit_bias, branch_bias)))

    def step(total, pair):
        sequence, seq_cot = pair
        result, pullback = jax.vjp(forward, sequence.astype(jnp.float32), params)
        seq_grad, param_grads = pullback(seq_cot.astype(jnp.float32))
        total = jax.tree.map(jnp.add, total, param_grads)
        return (total, (result.astype(jnp.bfloat16), seq_grad))
    zeros = jax.tree.map(jnp.zeros_like, params)
    total, (mixed, token_grad) = lax.scan(step, zeros, (tokens, cotangent))
    return (mixed, token_grad, total[0], total[1], total[2], total[3], total[4], total[5], total[6], total[7], total[8])
```

```python
from functools import partial

import jax
import jax.numpy as jnp
from jax import lax
from jax.sharding import PartitionSpec as P

HEAD_DIM = 64
EPS = 1e-05
BF = jnp.bfloat16
F32 = jnp.float32
GRID = ("dp", "ctx")


def matmul(left, right):
    return jnp.dot(left, right, preferred_element_type=F32)


def matmul_t(left, right):
    return lax.dot_general(left, right, (((1,), (1,)), ((), ())), preferred_element_type=F32)


def matmul_tn(left, right):
    return lax.dot_general(left, right, (((0,), (0,)), ((), ())), preferred_element_type=F32)


def normalize_fwd(value, gain, shift):
    mean = jnp.mean(value, axis=-1, keepdims=True)
    centred = value - mean
    variance = jnp.mean(centred * centred, axis=-1, keepdims=True)
    inverse = lax.rsqrt(variance + EPS)
    scaled = centred * inverse
    return (scaled * gain + shift, scaled, inverse)


def normalize_back(grad, scaled, inverse, gain):
    weighted = grad * gain
    first = jnp.mean(weighted, axis=-1, keepdims=True)
    second = jnp.mean(weighted * scaled, axis=-1, keepdims=True)
    return (
        inverse * (weighted - first - scaled * second),
        jnp.sum(grad * scaled, axis=0),
        jnp.sum(grad, axis=0),
    )


def split_heads(block):
    rows, width = block.shape
    heads = width // HEAD_DIM
    return block.reshape(rows, heads, HEAD_DIM).transpose(1, 0, 2)


def join_heads(block):
    heads, rows, depth = block.shape
    return block.transpose(1, 0, 2).reshape(rows, heads * depth)


def shifted(size, step):
    return [(i, (i + step) % size) for i in range(size)]


def gather_rows(own):
    size = lax.axis_size("mp")
    parts = [lax.ppermute(own, "mp", shifted(size, -step)) for step in range(1, size)]
    return jnp.concatenate([own, *parts], axis=0)


def scatter_rows(partial_sum):
    size = lax.axis_size("mp")
    share = partial_sum.shape[0] // size
    total = partial_sum[:share]
    for step in range(1, size):
        part = partial_sum[step * share : (step + 1) * share].astype(BF)
        total = total + lax.ppermute(part, "mp", shifted(size, step)).astype(F32)
    return total


def swap(value):
    return lax.ppermute(value, "ctx", [(0, 1), (1, 0)])


def masked_scores(query, keys, row_at, col_at):
    scores = matmul_t(query, keys) * HEAD_DIM ** (-0.5)
    return jnp.where(col_at[None, :] <= row_at[:, None], scores, -1e30)


def attend_forward(query, keys, values, row_at, col_at):
    def one_block(block):
        part_q, part_k, part_v = block
        scores = masked_scores(part_q, part_k, row_at, col_at)
        top = jnp.max(scores, axis=-1, keepdims=True)
        expo = jnp.exp(scores - top)
        total = jnp.sum(expo, axis=-1, keepdims=True)
        weights = (expo / total).astype(BF)
        return (matmul(weights, part_v), (top + jnp.log(total))[:, 0])

    outputs, logsum = lax.map(one_block, (split_heads(query), split_heads(keys), split_heads(values)))
    return (join_heads(outputs), logsum)


def attend_backward(query, keys, values, d_mixed, logsum, row_at, col_at):
    scale = HEAD_DIM ** (-0.5)

    def one_block(block):
        part_q, part_k, part_v, part_g, part_l = block
        scores = masked_scores(part_q, part_k, row_at, col_at)
        weights = jnp.exp(scores - part_l[:, None])
        d_weights = matmul_t(part_g, part_v)
        inner = jnp.sum(weights * d_weights, axis=-1, keepdims=True)
        d_scores = (weights * (d_weights - inner)).astype(BF)
        d_query = matmul(d_scores, part_k) * scale
        d_keys = matmul_tn(d_scores, part_q) * scale
        d_values = matmul_tn(weights.astype(BF), part_g)
        return (d_query, d_keys, d_values)

    grads = lax.map(
        one_block,
        (split_heads(query), split_heads(keys), split_heads(values), split_heads(d_mixed), logsum),
    )
    return tuple(join_heads(g) for g in grads)


def spread(shard):
    size = lax.axis_size(GRID)
    copies = jnp.broadcast_to(shard[None], (size, *shard.shape))
    return lax.all_to_all(copies, GRID, 0, 0, tiled=True).reshape(size * shard.shape[0], shard.shape[1])


def collect(grad):
    size = lax.axis_size(GRID)
    parts = grad.reshape(size, grad.shape[0] // size, grad.shape[1])
    return jnp.sum(lax.all_to_all(parts, GRID, 0, 0, tiled=True).astype(F32), axis=0)


def sum_over(value, axis, size, stride):
    block = 2 * stride
    pairs = [(i, (i // block) * block + (i + stride) % block) for i in range(size)]
    return value + lax.ppermute(value, axis, pairs)


def on_device(
    tokens,
    attn_in,
    attn_out,
    mlp_in,
    mlp_out,
    norm_gain,
    norm_shift,
    head_bias,
    unit_bias,
    branch_bias,
    cotangent,
):
    _, rows, width = tokens.shape
    layers, shard, _, local_w = attn_in.shape
    local_f = mlp_in.shape[2]
    ranks = lax.axis_size("mp")
    rank = lax.axis_index("mp")
    half = lax.axis_index("ctx")
    share = rows // ranks

    def rotated(block):
        return lax.dynamic_slice_in_dim(jnp.concatenate([block, block], axis=0), rank * share, rows, 0)

    def restored(block):
        start = rows - rank * share
        return lax.dynamic_slice_in_dim(jnp.concatenate([block, block], axis=0), start, rows, 0)

    at = jnp.arange(rows)
    place = (at + rank * share) % rows
    row_at = half * rows + place
    col_at = jnp.concatenate([row_at, (1 - half) * rows + place])

    flat_in = attn_in.reshape(layers, shard, 3 * local_w)
    first = spread(jnp.concatenate([flat_in[0], attn_out[0]], axis=1))
    packed = jnp.concatenate(
        [mlp_in[0], mlp_out[0], flat_in[1], attn_out[1], mlp_in[1], mlp_out[1]], axis=1
    )
    rest = lax.all_gather(packed, GRID, axis=0, tiled=True)
    at_f = 2 * local_f
    weights = [
        (
            first[:, : 3 * local_w],
            first[:, 3 * local_w :],
            rest[:, :local_f],
            rest[:, local_f:at_f],
        ),
        (
            rest[:, at_f : at_f + 3 * local_w],
            rest[:, at_f + 3 * local_w : at_f + 4 * local_w],
            rest[:, at_f + 4 * local_w : at_f + 4 * local_w + local_f],
            rest[:, at_f + 4 * local_w + local_f :],
        ),
    ]

    low_tokens = rotated(tokens.reshape(rows, width))
    state = low_tokens[:share].astype(F32)
    saved = []
    for layer in range(layers):
        w_in, w_out, w_up, w_down = weights[layer]
        if layer == 0:
            normed, scaled_all, inv_all = normalize_fwd(
                low_tokens.astype(F32), norm_gain[layer, 0], norm_shift[layer, 0]
            )
            a_low, a_scaled, a_inv = normed.astype(BF), scaled_all[:share], inv_all[:share]
        else:
            normed, a_scaled, a_inv = normalize_fwd(state, norm_gain[layer, 0], norm_shift[layer, 0])
            a_low = gather_rows(normed.astype(BF))
        projected = matmul(a_low, w_in)
        query = (projected[:, :local_w] + head_bias[layer, 0]).astype(BF)
        keys = projected[:, local_w : 2 * local_w].astype(BF)
        values = (projected[:, 2 * local_w :] + head_bias[layer, 1]).astype(BF)
        both = jnp.concatenate([keys, values], axis=1)
        both = jnp.concatenate([both, swap(both)], axis=0)
        key_all, value_all = both[:, :local_w], both[:, local_w:]
        heads_out, logsum = attend_forward(query, key_all, value_all, row_at, col_at)
        heads_low = heads_out.astype(BF)
        middle = state + scatter_rows(matmul_t(heads_low, w_out)) + branch_bias[layer, 0]
        second, c_scaled, c_inv = normalize_fwd(middle, norm_gain[layer, 1], norm_shift[layer, 1])
        c_low = gather_rows(second.astype(BF))
        hidden = matmul(c_low, w_up) + unit_bias[layer]
        active = jax.nn.gelu(hidden, approximate=True).astype(BF)
        state = middle + scatter_rows(matmul_t(active, w_down)) + branch_bias[layer, 1]
        saved.append(
            (a_low, a_scaled, a_inv, query, key_all, value_all, logsum, heads_low)
            + (c_low, c_scaled, c_inv, hidden, active)
        )
    mixed = lax.all_gather(state.astype(BF), "mp", axis=0, tiled=True)

    grad_low = rotated(cotangent.reshape(rows, width))
    grad = grad_low[:share].astype(F32)
    gains, shifts, heads_b, units_b, branches_b, matrices = {}, {}, {}, {}, {}, {}
    for layer in reversed(range(layers)):
        w_in, w_out, w_up, w_down = weights[layer]
        a_low, a_scaled, a_inv, query, key_all, value_all, logsum, heads_low = saved[layer][:8]
        c_low, c_scaled, c_inv, hidden, active = saved[layer][8:]
        if layer < layers - 1:
            grad_low = gather_rows(grad.astype(BF))
        bias_down = jnp.sum(grad, axis=0)
        grad_down = matmul_tn(grad_low, active).astype(BF)
        d_active = matmul(grad_low, w_down)
        gelu_pull = jax.vjp(partial(jax.nn.gelu, approximate=True), hidden)[1]
        d_hidden = gelu_pull(d_active)[0]
        units_b[layer] = jnp.sum(d_hidden, axis=0)
        hidden_low = d_hidden.astype(BF)
        grad_up = matmul_tn(c_low, hidden_low).astype(BF)
        d_second = scatter_rows(matmul_t(hidden_low, w_up))
        d_middle, gain_two, shift_two = normalize_back(d_second, c_scaled, c_inv, norm_gain[layer, 1])
        grad_mid = grad + d_middle
        bias_attn = jnp.sum(grad_mid, axis=0)
        mid_low = gather_rows(grad_mid.astype(BF))
        grad_out = matmul_tn(mid_low, heads_low).astype(BF)
        d_heads = matmul(mid_low, w_out).astype(BF)
        d_query, d_keys_all, d_values_all = attend_backward(
            query, key_all, value_all, d_heads, logsum, row_at, col_at
        )
        d_both = jnp.concatenate([d_keys_all, d_values_all], axis=1)
        d_both = d_both[:rows] + swap(d_both[rows:].astype(BF)).astype(F32)
        heads_b[layer] = jnp.stack([jnp.sum(d_query, axis=0), jnp.sum(d_both[:, local_w:], axis=0)])
        d_projected = jnp.concatenate([d_query, d_both], axis=1).astype(BF)
        grad_in = matmul_tn(a_low, d_projected).astype(BF)
        d_normed = scatter_rows(matmul_t(d_projected, w_in))
        d_state, gain_one, shift_one = normalize_back(d_normed, a_scaled, a_inv, norm_gain[layer, 0])
        grad = grad_mid + d_state
        matrices[layer] = (grad_in, grad_out, grad_up, grad_down)
        gains[layer] = jnp.stack([gain_one, gain_two])
        shifts[layer] = jnp.stack([shift_one, shift_two])
        branches_b[layer] = jnp.stack([bias_attn, bias_down])

    def reduced(parts):
        packed = jnp.concatenate(parts, axis=1)
        return lax.psum_scatter(packed, GRID, scatter_dimension=0, tiled=True).astype(F32)

    early = reduced([matrices[1][2], matrices[1][3]])
    later = reduced([matrices[1][0], matrices[1][1], matrices[0][2], matrices[0][3]])
    last = collect(jnp.concatenate([matrices[0][0], matrices[0][1]], axis=1))
    w3, w4 = 3 * local_w, 4 * local_w
    all_in = jnp.stack([last[:, :w3], later[:, :w3]]).reshape(layers, shard, 3, local_w)
    all_out = jnp.stack([last[:, w3:], later[:, w3:w4]])
    all_up = jnp.stack([later[:, w4 : w4 + local_f], early[:, :local_f]])
    all_down = jnp.stack([later[:, w4 + local_f :], early[:, local_f:]])

    def ordered(items):
        return jnp.stack([items[layer] for layer in range(layers)])

    shared = jnp.stack([ordered(gains), ordered(shifts), ordered(branches_b)]).reshape(-1)
    shared = sum_over(shared, "mp", ranks, 1)
    shared = sum_over(shared, "mp", ranks, 2)
    sides = jnp.concatenate([ordered(heads_b).reshape(-1), ordered(units_b).reshape(-1)])
    vector = jnp.concatenate([shared, sides]).reshape(-1, 128)
    vector = sum_over(vector, "ctx", 2, 1)
    dp = lax.axis_size("dp")
    stride = 1
    while stride < dp:
        vector = sum_over(vector, "dp", dp, stride)
        stride *= 2
    vector = vector.reshape(-1)
    cut = shared.shape[0]
    shared = vector[:cut].reshape(3, layers, 2, width)
    head_grad = vector[cut : cut + layers * 2 * local_w].reshape(layers, 2, local_w)
    unit_grad = vector[cut + layers * 2 * local_w :].reshape(layers, local_f)

    token_grad = restored(gather_rows(grad.astype(BF))).astype(F32)
    return (
        mixed.reshape(1, rows, width),
        token_grad.reshape(1, rows, width),
        all_in,
        all_out,
        all_up,
        all_down,
        shared[0],
        shared[1],
        head_grad,
        unit_grad,
        shared[2],
    )


def solution(mesh):
    return jax.shard_map(
        on_device,
        mesh=mesh,
        in_specs=(
            P("dp", "ctx", None),
            P(None, ("dp", "ctx"), None, "mp"),
            P(None, ("dp", "ctx"), "mp"),
            P(None, ("dp", "ctx"), "mp"),
            P(None, ("dp", "ctx"), "mp"),
            P(),
            P(),
            P(None, None, "mp"),
            P(None, "mp"),
            P(),
            P("dp", "ctx", None),
        ),
        out_specs=(
            P("dp", "ctx", None),
            P("dp", "ctx", None),
            P(None, ("dp", "ctx"), None, "mp"),
            P(None, ("dp", "ctx"), "mp"),
            P(None, ("dp", "ctx"), "mp"),
            P(None, ("dp", "ctx"), "mp"),
            P(),
            P(),
            P(None, None, "mp"),
            P(None, "mp"),
            P(),
        ),
        check_vma=False,
    )
```

```python
from functools import partial

import jax
import jax.numpy as jnp
from jax import lax
from jax.experimental import pallas as pl
from jax.experimental.pallas import tpu as pltpu
from jax.sharding import PartitionSpec as P

HEAD_DIM = 64
EPS = 1e-05
BF = jnp.bfloat16
F32 = jnp.float32
GRID = ("dp", "ctx")
LOG2E = 1.4426950408889634


def matmul(left, right):
    return jnp.dot(left, right, preferred_element_type=F32)


def matmul_t(left, right):
    return lax.dot_general(left, right, (((1,), (1,)), ((), ())), preferred_element_type=F32)


def matmul_tn(left, right):
    return lax.dot_general(left, right, (((0,), (0,)), ((), ())), preferred_element_type=F32)


def normalize_fwd(value, gain, shift):
    mean = jnp.mean(value, axis=-1, keepdims=True)
    centred = value - mean
    variance = jnp.mean(centred * centred, axis=-1, keepdims=True)
    inverse = lax.rsqrt(variance + EPS)
    scaled = centred * inverse
    return (scaled * gain + shift, scaled, inverse)


def normalize_back(grad, scaled, inverse, gain):
    weighted = grad * gain
    first = jnp.mean(weighted, axis=-1, keepdims=True)
    second = jnp.mean(weighted * scaled, axis=-1, keepdims=True)
    return (
        inverse * (weighted - first - scaled * second),
        jnp.sum(grad * scaled, axis=0),
        jnp.sum(grad, axis=0),
    )


def head_lanes(block, head):
    lane = lax.broadcasted_iota(jnp.int32, block.shape, 1)
    return jnp.where((lane >= HEAD_DIM) == (head == 1), block, jnp.zeros_like(block))


def attend_kernel(half_ref, mask_ref, q_ref, own_ref, far_ref, o_ref, lse_ref):
    factor = HEAD_DIM ** (-0.5) * LOG2E

    def run(far):
        out = None
        for head in range(2):
            query = head_lanes(q_ref[...], head)
            near_s = matmul_t(own_ref[0], query) * factor + mask_ref[...]
            top = jnp.max(near_s, axis=0, keepdims=True)
            if far:
                far_s = matmul_t(far_ref[0], query) * factor
                top = jnp.maximum(top, jnp.max(far_s, axis=0, keepdims=True))
            near_p = jnp.exp2(near_s - top)
            total = jnp.sum(near_p, axis=0, keepdims=True)
            mixed = matmul_tn(head_lanes(own_ref[1], head), near_p.astype(BF))
            if far:
                far_p = jnp.exp2(far_s - top)
                total = total + jnp.sum(far_p, axis=0, keepdims=True)
                mixed = mixed + matmul_tn(head_lanes(far_ref[1], head), far_p.astype(BF))
            lse_ref[0, head : head + 1, :] = top + jnp.log2(total)
            mixed = mixed / total
            out = mixed if out is None else out + mixed
        o_ref[...] = out.T.astype(BF)

    pl.when(half_ref[0] == 1)(lambda: run(True))
    pl.when(half_ref[0] == 0)(lambda: run(False))


def attend_back_kernel(
    half_ref, mask_ref, q_ref, own_ref, far_ref, g_ref, lse_ref, dq_ref, down_ref, dfar_ref
):
    scale = HEAD_DIM ** (-0.5)
    factor = scale * LOG2E

    def run(far):
        refs = [own_ref] + ([far_ref] if far else [])
        d_query, d_keys, d_values = None, [None, None], [None, None]
        for head in range(2):
            query, grad = head_lanes(q_ref[...], head), head_lanes(g_ref[...], head)
            lse = lse_ref[0, head : head + 1, :]
            weights, d_weights, inner = [], [], None
            for index, ref in enumerate(refs):
                scores = matmul_t(ref[0], query) * factor - lse
                if index == 0:
                    scores = scores + mask_ref[...]
                weights.append(jnp.exp2(scores))
                d_weights.append(matmul_t(ref[1], grad))
                part = jnp.sum(weights[-1] * d_weights[-1], axis=0, keepdims=True)
                inner = part if inner is None else inner + part
            for index, ref in enumerate(refs):
                d_scores = (weights[index] * (d_weights[index] - inner)).astype(BF)
                part_k = matmul(d_scores, query)
                part_v = matmul(weights[index].astype(BF), grad)
                part_q = matmul_tn(head_lanes(ref[0], head), d_scores)
                d_keys[index] = part_k if d_keys[index] is None else d_keys[index] + part_k
                d_values[index] = part_v if d_values[index] is None else d_values[index] + part_v
                d_query = part_q if d_query is None else d_query + part_q
        dq_ref[...] = d_query.T * scale
        down_ref[0] = d_keys[0] * scale
        down_ref[1] = d_values[0]
        if far:
            dfar_ref[0] = (d_keys[1] * scale).astype(BF)
            dfar_ref[1] = d_values[1].astype(BF)
        else:
            dfar_ref[...] = jnp.zeros(dfar_ref.shape, BF)

    pl.when(half_ref[0] == 1)(lambda: run(True))
    pl.when(half_ref[0] == 0)(lambda: run(False))


def attend_specs(rows):
    pair = 2 * HEAD_DIM
    return (
        pl.BlockSpec(memory_space=pltpu.SMEM),
        pl.BlockSpec((rows, rows), lambda i: (0, 0)),
        pl.BlockSpec((rows, pair), lambda i: (0, i)),
        pl.BlockSpec((2, rows, pair), lambda i: (0, 0, i)),
        pl.BlockSpec((1, 2, rows), lambda i: (i, 0, 0)),
    )


def kernel_params(flops, moved):
    return dict(
        compiler_params=pltpu.CompilerParams(vmem_limit_bytes=40 * 1024 * 1024),
        cost_estimate=pl.CostEstimate(flops=flops, bytes_accessed=moved, transcendentals=0),
    )


def attend_forward(half, mask, query, own, far):
    rows, width = query.shape
    pairs = width // (2 * HEAD_DIM)
    scalar, square, flat, both, line = attend_specs(rows)
    return pl.pallas_call(
        attend_kernel,
        grid=(pairs,),
        in_specs=[scalar, square, flat, both, both],
        out_specs=[flat, line],
        out_shape=[
            jax.ShapeDtypeStruct((rows, width), BF),
            jax.ShapeDtypeStruct((pairs, 2, rows), F32),
        ],
        **kernel_params(8000000000, 4000000),
    )(half, mask, query, own, far)


def attend_backward(half, mask, query, own, far, grad, lse):
    rows, width = query.shape
    pairs = width // (2 * HEAD_DIM)
    scalar, square, flat, both, line = attend_specs(rows)
    return pl.pallas_call(
        attend_back_kernel,
        grid=(pairs,),
        in_specs=[scalar, square, flat, both, both, flat, line],
        out_specs=[flat, both, both],
        out_shape=[
            jax.ShapeDtypeStruct((rows, width), F32),
            jax.ShapeDtypeStruct((2, rows, width), F32),
            jax.ShapeDtypeStruct((2, rows, width), BF),
        ],
        **kernel_params(14000000000, 6000000),
    )(half, mask, query, own, far, grad, lse)


def product_kernel(count, *refs):
    out_ref, at = refs[-1], 0
    for n in range(count):
        width = refs[2 * n + 1].shape[1]
        out_ref[:, at : at + width] = matmul_tn(refs[2 * n][...], refs[2 * n + 1][...]).astype(BF)
        at += width
    if len(refs) > 2 * count + 1:
        out_ref[:, at:] = refs[2 * count][...]


def weight_products(pairs, extra=None):
    rows, height = pairs[0][0].shape
    tile = 256
    specs, operands, width = [], [], 0
    for left, right in pairs:
        specs += [
            pl.BlockSpec((rows, tile), lambda i: (0, i)),
            pl.BlockSpec((rows, right.shape[1]), lambda i: (0, 0)),
        ]
        operands += [left, right]
        width += right.shape[1]
    flops = 2 * rows * height * width
    if extra is not None:
        specs.append(pl.BlockSpec((tile, extra.shape[1]), lambda i: (i, 0)))
        operands.append(extra)
        width += extra.shape[1]
    return pl.pallas_call(
        partial(product_kernel, len(pairs)),
        grid=(height // tile,),
        in_specs=specs,
        out_specs=pl.BlockSpec((tile, width), lambda i: (i, 0)),
        out_shape=jax.ShapeDtypeStruct((height, width), BF),
        **kernel_params(flops, 2 * (height * width + rows * (width + len(pairs) * height))),
    )(*operands)


def shifted(size, step):
    return [(i, (i + step) % size) for i in range(size)]


def gather_rows(own):
    size = lax.axis_size("mp")
    parts = [lax.ppermute(own, "mp", shifted(size, -step)) for step in range(1, size)]
    return jnp.concatenate([own, *parts], axis=0)


def scatter_rows(partial_sum):
    size = lax.axis_size("mp")
    share = partial_sum.shape[0] // size
    total = partial_sum[:share]
    for step in range(1, size):
        part = partial_sum[step * share : (step + 1) * share].astype(BF)
        total = total + lax.ppermute(part, "mp", shifted(size, step)).astype(F32)
    return total


def swap(value):
    return lax.ppermute(value, "ctx", [(0, 1), (1, 0)])


def spread(shard):
    size = lax.axis_size(GRID)
    copies = jnp.broadcast_to(shard[None], (size, *shard.shape))
    return lax.all_to_all(copies, GRID, 0, 0, tiled=True).reshape(size * shard.shape[0], shard.shape[1])


def exchange(value):
    size = lax.axis_size(GRID)
    parts = value.reshape(size, value.shape[0] // size, value.shape[1])
    return lax.all_to_all(parts, GRID, 0, 0, tiled=True)


def sum_ranks(value):
    size = lax.axis_size("mp")
    parts = [value] + [lax.ppermute(value, "mp", shifted(size, -step)) for step in range(1, size)]
    start = lax.rem(size - lax.axis_index("mp"), size)
    return jnp.sum(lax.dynamic_slice_in_dim(jnp.stack(parts + parts), start, size, 0), axis=0)


def on_device(
    tokens,
    attn_in,
    attn_out,
    mlp_in,
    mlp_out,
    norm_gain,
    norm_shift,
    head_bias,
    unit_bias,
    branch_bias,
    cotangent,
):
    _, rows, width = tokens.shape
    layers, shard, _, local_w = attn_in.shape
    local_f = mlp_in.shape[2]
    ranks = lax.axis_size("mp")
    rank = lax.axis_index("mp")
    half = lax.axis_index("ctx")
    share = rows // ranks

    def rotated(block):
        return lax.dynamic_slice_in_dim(jnp.concatenate([block, block], axis=0), rank * share, rows, 0)

    def restored(block):
        start = rows - rank * share
        return lax.dynamic_slice_in_dim(jnp.concatenate([block, block], axis=0), start, rows, 0)

    place = (jnp.arange(rows) + rank * share) % rows
    mask = jnp.where(place[:, None] <= place[None, :], 0.0, -1e30).astype(F32)
    half = half.reshape(1)

    flat_in = attn_in.reshape(layers, shard, 3 * local_w)
    first = spread(flat_in[0])
    packed = jnp.concatenate([attn_out[0], mlp_in[0], mlp_out[0]], axis=1)
    near = lax.all_gather(packed, GRID, axis=0, tiled=True)
    packed = jnp.concatenate([flat_in[1], attn_out[1], mlp_in[1], mlp_out[1]], axis=1)
    rest = lax.all_gather(packed, GRID, axis=0, tiled=True)
    w3, w4 = 3 * local_w, 4 * local_w
    weights = [
        (first, near[:, :local_w], near[:, local_w : local_w + local_f], near[:, local_w + local_f :]),
        (rest[:, :w3], rest[:, w3:w4], rest[:, w4 : w4 + local_f], rest[:, w4 + local_f :]),
    ]

    low_tokens = rotated(tokens.reshape(rows, width))
    state = low_tokens[:share].astype(F32)
    saved = []
    for layer in range(layers):
        w_in, w_out, w_up, w_down = weights[layer]
        if layer == 0:
            normed, scaled_all, inv_all = normalize_fwd(
                low_tokens.astype(F32), norm_gain[layer, 0], norm_shift[layer, 0]
            )
            a_low, a_scaled, a_inv = normed.astype(BF), scaled_all[:share], inv_all[:share]
            first_scaled = scaled_all
        else:
            normed, a_scaled, a_inv = normalize_fwd(state, norm_gain[layer, 0], norm_shift[layer, 0])
            a_low = gather_rows(normed.astype(BF))
        projected = matmul(a_low, w_in)
        query = (projected[:, :local_w] + head_bias[layer, 0]).astype(BF)
        keys = projected[:, local_w : 2 * local_w].astype(BF)
        values = (projected[:, 2 * local_w :] + head_bias[layer, 1]).astype(BF)
        own = jnp.stack([keys, values])
        far = swap(own)
        heads_low, logsum = attend_forward(half, mask, query, own, far)
        middle = state + scatter_rows(matmul_t(heads_low, w_out)) + branch_bias[layer, 0]
        second, c_scaled, c_inv = normalize_fwd(middle, norm_gain[layer, 1], norm_shift[layer, 1])
        c_low = gather_rows(second.astype(BF))
        hidden = matmul(c_low, w_up) + unit_bias[layer]
        active = jax.nn.gelu(hidden, approximate=True).astype(BF)
        state = middle + scatter_rows(matmul_t(active, w_down)) + branch_bias[layer, 1]
        saved.append(
            (a_low, a_scaled, a_inv, query, own, far, logsum, heads_low)
            + (c_low, c_scaled, c_inv, hidden, active)
        )
    grad_low = rotated(cotangent.reshape(rows, width))
    grad = grad_low[:share].astype(F32)
    gains, shifts, heads_b, units_b, branches_b, matrices = {}, {}, {}, {}, {}, {}
    size = lax.axis_size(GRID)
    for layer in reversed(range(layers)):
        w_in, w_out, w_up, w_down = weights[layer]
        a_low, a_scaled, a_inv, query, own, far, logsum, heads_low = saved[layer][:8]
        c_low, c_scaled, c_inv, hidden, active = saved[layer][8:]
        if layer < layers - 1:
            grad_low = gather_rows(grad.astype(BF))
        bias_down = jnp.sum(grad, axis=0)
        d_active = matmul(grad_low, w_down)
        gelu_pull = jax.vjp(partial(jax.nn.gelu, approximate=True), hidden)[1]
        d_hidden = gelu_pull(d_active)[0]
        units_b[layer] = jnp.sum(d_hidden, axis=0)
        hidden_low = d_hidden.astype(BF)
        mlp_pairs = [(c_low, hidden_low), (grad_low, active)]
        if layer == layers - 1:
            early = weight_products(mlp_pairs)
        else:
            later = weight_products(attn_pairs + mlp_pairs)
        d_second = scatter_rows(matmul_t(hidden_low, w_up))
        d_middle, gain_two, shift_two = normalize_back(d_second, c_scaled, c_inv, norm_gain[layer, 1])
        grad_mid = grad + d_middle
        bias_attn = jnp.sum(grad_mid, axis=0)
        branches_b[layer] = jnp.stack([bias_attn, bias_down])
        mid_low = gather_rows(grad_mid.astype(BF))
        d_heads = matmul(mid_low, w_out).astype(BF)
        if layer == layers - 1:
            d_heads, state_low = lax.optimization_barrier((d_heads, state.astype(BF)))
            mixed = restored(gather_rows(state_low))
        else:
            ready = jnp.concatenate(
                [gains[1], shifts[1], gain_two[None], shift_two[None], branches_b[0], branches_b[1]]
            ).reshape(-1)
            shared_size = ready.shape[0]
            ready = jnp.concatenate([ready, heads_b[1].reshape(-1), units_b[0], units_b[1]])
            chunk = ready.shape[0] // size
            block = 128 * shard
            ready = jnp.pad(ready.reshape(size, chunk), ((0, 0), (0, block - chunk)))
            extra = ready.astype(BF).reshape(size * shard, 128)
            moved = jnp.sum(exchange(weight_products([(mid_low, heads_low)], extra)).astype(F32), axis=0)
            grad_out_first = moved[:, :local_w]
            ready = moved[:, local_w:].reshape(-1)[:chunk]
        d_query, d_own, d_far = attend_backward(half, mask, query, own, far, d_heads, logsum)
        d_own = d_own + swap(d_far).astype(F32)
        heads_b[layer] = jnp.stack([jnp.sum(d_query, axis=0), jnp.sum(d_own[1], axis=0)])
        d_projected = jnp.concatenate([d_query, d_own[0], d_own[1]], axis=1).astype(BF)
        d_partial = matmul_t(d_projected, w_in)
        if layer == layers - 1:
            attn_pairs = [(a_low, d_projected), (mid_low, heads_low)]
        else:
            late = jnp.concatenate(
                [
                    jnp.sum(d_partial * first_scaled, axis=0),
                    jnp.sum(d_partial, axis=0),
                    heads_b[0].reshape(-1),
                    ready,
                ]
            )
            extra = jnp.pad(late, (0, block - late.shape[0])).astype(BF).reshape(shard, 128)
            extra = jnp.broadcast_to(extra[None], (size, shard, 128)).reshape(size * shard, 128)
            moved = exchange(weight_products([(a_low, d_projected)], extra))
            grad_in_first = jnp.sum(moved[:, :, :w3].astype(F32), axis=0)
            extra = moved[:, :, w3:].reshape(size, block).astype(F32)
        d_normed = scatter_rows(d_partial)
        d_state, gain_one, shift_one = normalize_back(d_normed, a_scaled, a_inv, norm_gain[layer, 0])
        grad = grad_mid + d_state
        gains[layer] = jnp.stack([gain_one, gain_two])
        shifts[layer] = jnp.stack([shift_one, shift_two])

    def reduced(packed):
        return lax.psum_scatter(packed, GRID, scatter_dimension=0, tiled=True).astype(F32)

    early, later = reduced(early), reduced(later)
    all_in = jnp.stack([grad_in_first, later[:, :w3]]).reshape(layers, shard, 3, local_w)
    all_out = jnp.stack([grad_out_first, later[:, w3:w4]])
    all_up = jnp.stack([later[:, w4 : w4 + local_f], early[:, :local_f]])
    all_down = jnp.stack([later[:, w4 + local_f :], early[:, local_f:]])

    late_size = late.shape[0] - chunk
    late = jnp.sum(extra[:, :late_size], axis=0)
    ready = extra[:, late_size : late_size + chunk].reshape(-1)
    shared = sum_ranks(jnp.concatenate([ready[:shared_size], late[: 2 * width]]).reshape(-1, 128))
    shared = shared.reshape(-1, width)
    gain_grad = jnp.stack([shared[10], shared[4], shared[0], shared[1]]).reshape(layers, 2, width)
    shift_grad = jnp.stack([shared[11], shared[5], shared[2], shared[3]]).reshape(layers, 2, width)
    branch_grad = shared[6:10].reshape(layers, 2, width)
    cut = shared_size + 2 * local_w
    head_grad = jnp.concatenate([late[2 * width :], ready[shared_size:cut]]).reshape(layers, 2, local_w)
    unit_grad = ready[cut : cut + layers * local_f].reshape(layers, local_f)

    token_grad = restored(gather_rows(grad.astype(BF))).astype(F32)
    return (
        mixed.reshape(1, rows, width),
        token_grad.reshape(1, rows, width),
        all_in,
        all_out,
        all_up,
        all_down,
        gain_grad,
        shift_grad,
        head_grad,
        unit_grad,
        branch_grad,
    )


def solution(mesh):
    return jax.shard_map(
        on_device,
        mesh=mesh,
        in_specs=(
            P("dp", "ctx", None),
            P(None, ("dp", "ctx"), None, "mp"),
            P(None, ("dp", "ctx"), "mp"),
            P(None, ("dp", "ctx"), "mp"),
            P(None, ("dp", "ctx"), "mp"),
            P(),
            P(),
            P(None, None, "mp"),
            P(None, "mp"),
            P(),
            P("dp", "ctx", None),
        ),
        out_specs=(
            P("dp", "ctx", None),
            P("dp", "ctx", None),
            P(None, ("dp", "ctx"), None, "mp"),
            P(None, ("dp", "ctx"), "mp"),
            P(None, ("dp", "ctx"), "mp"),
            P(None, ("dp", "ctx"), "mp"),
            P(),
            P(),
            P(None, None, "mp"),
            P(None, "mp"),
            P(),
        ),
        check_vma=False,
    )
```

```python
from functools import partial

import jax
import jax.numpy as jnp
from jax import lax
from jax.experimental import pallas as pl
from jax.experimental.pallas import tpu as pltpu
from jax.sharding import PartitionSpec as P

HEAD_DIM = 64
EPS = 1e-05
BF = jnp.bfloat16
F32 = jnp.float32
GRID = ("dp", "ctx")
LOG2E = 1.4426950408889634


def matmul(left, right):
    return jnp.dot(left, right, preferred_element_type=F32)


def matmul_t(left, right):
    return lax.dot_general(left, right, (((1,), (1,)), ((), ())), preferred_element_type=F32)


def matmul_tn(left, right):
    return lax.dot_general(left, right, (((0,), (0,)), ((), ())), preferred_element_type=F32)


def normalize_fwd(value, gain, shift):
    mean = jnp.mean(value, axis=-1, keepdims=True)
    centred = value - mean
    variance = jnp.mean(centred * centred, axis=-1, keepdims=True)
    inverse = lax.rsqrt(variance + EPS)
    scaled = centred * inverse
    return (scaled * gain + shift, scaled, inverse)


def normalize_back(grad, scaled, inverse, gain):
    weighted = grad * gain
    first = jnp.mean(weighted, axis=-1, keepdims=True)
    second = jnp.mean(weighted * scaled, axis=-1, keepdims=True)
    return (
        inverse * (weighted - first - scaled * second),
        jnp.sum(grad * scaled, axis=0),
        jnp.sum(grad, axis=0),
    )


def head_lanes(block, head):
    lane = lax.broadcasted_iota(jnp.int32, block.shape, 1)
    return jnp.where((lane >= HEAD_DIM) == (head == 1), block, jnp.zeros_like(block))


def attend_kernel(half_ref, mask_ref, q_ref, own_ref, far_ref, o_ref, lse_ref):
    factor = HEAD_DIM ** (-0.5) * LOG2E

    def run(far):
        out = None
        for head in range(2):
            query = head_lanes(q_ref[...], head)
            near_s = matmul_t(own_ref[0], query) * factor + mask_ref[...]
            top = jnp.max(near_s, axis=0, keepdims=True)
            if far:
                far_s = matmul_t(far_ref[0], query) * factor
                top = jnp.maximum(top, jnp.max(far_s, axis=0, keepdims=True))
            near_p = jnp.exp2(near_s - top)
            total = jnp.sum(near_p, axis=0, keepdims=True)
            mixed = matmul_tn(head_lanes(own_ref[1], head), near_p.astype(BF))
            if far:
                far_p = jnp.exp2(far_s - top)
                total = total + jnp.sum(far_p, axis=0, keepdims=True)
                mixed = mixed + matmul_tn(head_lanes(far_ref[1], head), far_p.astype(BF))
            lse_ref[0, head : head + 1, :] = top + jnp.log2(total)
            mixed = mixed / total
            out = mixed if out is None else out + mixed
        o_ref[...] = out.T.astype(BF)

    pl.when(half_ref[0] == 1)(lambda: run(True))
    pl.when(half_ref[0] == 0)(lambda: run(False))


def attend_back_kernel(
    half_ref, mask_ref, q_ref, own_ref, far_ref, g_ref, lse_ref, dq_ref, down_ref, dfar_ref
):
    scale = HEAD_DIM ** (-0.5)
    factor = scale * LOG2E

    def run(far):
        refs = [own_ref] + ([far_ref] if far else [])
        d_query, d_keys, d_values = None, [None, None], [None, None]
        for head in range(2):
            query, grad = head_lanes(q_ref[...], head), head_lanes(g_ref[...], head)
            lse = lse_ref[0, head : head + 1, :]
            weights, d_weights, inner = [], [], None
            for index, ref in enumerate(refs):
                scores = matmul_t(ref[0], query) * factor - lse
                if index == 0:
                    scores = scores + mask_ref[...]
                weights.append(jnp.exp2(scores))
                d_weights.append(matmul_t(ref[1], grad))
                part = jnp.sum(weights[-1] * d_weights[-1], axis=0, keepdims=True)
                inner = part if inner is None else inner + part
            for index, ref in enumerate(refs):
                d_scores = (weights[index] * (d_weights[index] - inner)).astype(BF)
                part_k = matmul(d_scores, query)
                part_v = matmul(weights[index].astype(BF), grad)
                part_q = matmul_tn(head_lanes(ref[0], head), d_scores)
                d_keys[index] = part_k if d_keys[index] is None else d_keys[index] + part_k
                d_values[index] = part_v if d_values[index] is None else d_values[index] + part_v
                d_query = part_q if d_query is None else d_query + part_q
        dq_ref[...] = d_query.T * scale
        down_ref[0] = d_keys[0] * scale
        down_ref[1] = d_values[0]
        if far:
            dfar_ref[0] = (d_keys[1] * scale).astype(BF)
            dfar_ref[1] = d_values[1].astype(BF)
        else:
            dfar_ref[...] = jnp.zeros(dfar_ref.shape, BF)

    pl.when(half_ref[0] == 1)(lambda: run(True))
    pl.when(half_ref[0] == 0)(lambda: run(False))


def attend_specs(rows):
    pair = 2 * HEAD_DIM
    return (
        pl.BlockSpec(memory_space=pltpu.SMEM),
        pl.BlockSpec((rows, rows), lambda i: (0, 0)),
        pl.BlockSpec((rows, pair), lambda i: (0, i)),
        pl.BlockSpec((2, rows, pair), lambda i: (0, 0, i)),
        pl.BlockSpec((1, 2, rows), lambda i: (i, 0, 0)),
    )


def kernel_params(flops, moved):
    return dict(
        compiler_params=pltpu.CompilerParams(vmem_limit_bytes=40 * 1024 * 1024),
        cost_estimate=pl.CostEstimate(flops=flops, bytes_accessed=moved, transcendentals=0),
    )


def attend_forward(half, mask, query, own, far):
    rows, width = query.shape
    pairs = width // (2 * HEAD_DIM)
    scalar, square, flat, both, line = attend_specs(rows)
    return pl.pallas_call(
        attend_kernel,
        grid=(pairs,),
        in_specs=[scalar, square, flat, both, both],
        out_specs=[flat, line],
        out_shape=[
            jax.ShapeDtypeStruct((rows, width), BF),
            jax.ShapeDtypeStruct((pairs, 2, rows), F32),
        ],
        **kernel_params(1000000000, 4000000),
    )(half, mask, query, own, far)


def attend_backward(half, mask, query, own, far, grad, lse):
    rows, width = query.shape
    pairs = width // (2 * HEAD_DIM)
    scalar, square, flat, both, line = attend_specs(rows)
    return pl.pallas_call(
        attend_back_kernel,
        grid=(pairs,),
        in_specs=[scalar, square, flat, both, both, flat, line],
        out_specs=[flat, both, both],
        out_shape=[
            jax.ShapeDtypeStruct((rows, width), F32),
            jax.ShapeDtypeStruct((2, rows, width), F32),
            jax.ShapeDtypeStruct((2, rows, width), BF),
        ],
        **kernel_params(1000000000, 6000000),
    )(half, mask, query, own, far, grad, lse)


def product_kernel(counts, *refs):
    out_ref, at, column = refs[-1], 0, 0

    def taken(count):
        nonlocal at
        blocks = [ref[...] for ref in refs[at : at + count]]
        at += count
        return blocks[0] if count == 1 else jnp.concatenate(blocks, axis=0)

    for left_count, right_count in counts:
        left, right = taken(left_count), taken(right_count)
        width = right.shape[1]
        out_ref[:, column : column + width] = matmul_tn(left, right).astype(BF)
        column += width
    if at < len(refs) - 1:
        out_ref[:, column:] = refs[at][...]


def weight_products(pairs, extra=None):
    pairs = [[x if isinstance(x, list) else [x] for x in pair] for pair in pairs]
    height = pairs[0][0][0].shape[1]
    tile = 256
    specs, operands, width = [], [], 0
    for left, right in pairs:
        specs += [pl.BlockSpec((x.shape[0], tile), lambda i: (0, i)) for x in left]
        specs += [pl.BlockSpec(x.shape, lambda i: (0, 0)) for x in right]
        operands += [*left, *right]
        width += right[0].shape[1]
    if extra is not None:
        specs.append(pl.BlockSpec((tile, extra.shape[1]), lambda i: (i, 0)))
        operands.append(extra)
        width += extra.shape[1]
    return pl.pallas_call(
        partial(product_kernel, [(len(left), len(right)) for left, right in pairs]),
        grid=(height // tile,),
        in_specs=specs,
        out_specs=pl.BlockSpec((tile, width), lambda i: (i, 0)),
        out_shape=pltpu.HBM((height, width), BF),
        **kernel_params(1000000, 1000000),
    )(*operands)


def shifted(size, step):
    return [(i, (i + step) % size) for i in range(size)]


def gather_blocks(own):
    size = lax.axis_size("mp")
    return [own] + [lax.ppermute(own, "mp", shifted(size, -step)) for step in range(1, size)]


def gather_rows(own):
    return jnp.concatenate(gather_blocks(own), axis=0)


def return_blocks(blocks, beside=None):
    size = lax.axis_size("mp")
    parts = [
        lax.ppermute(blocks[step].astype(BF), "mp", shifted(size, step)) for step in range(1, size)
    ]
    if beside is not None:
        parts[1], beside = lax.optimization_barrier((parts[1], beside))
    total = blocks[0]
    for part in parts:
        total = total + part.astype(F32)
    return total if beside is None else (total, beside)


def by_rank(blocks):
    size = lax.axis_size("mp")
    start = lax.rem(size - lax.axis_index("mp"), size)
    return lax.dynamic_slice_in_dim(jnp.stack(blocks + blocks), start, size, 0)


def row_blocks(value):
    share = value.shape[0] // lax.axis_size("mp")
    return [value[at : at + share] for at in range(0, value.shape[0], share)]


def scatter_rows(partial_sum):
    return return_blocks(row_blocks(partial_sum))


def swap(value):
    return lax.ppermute(value, "ctx", [(0, 1), (1, 0)])


def spread(shard):
    size = lax.axis_size(GRID)
    copies = jnp.broadcast_to(shard[None], (size, *shard.shape))
    return lax.all_to_all(copies, GRID, 0, 0, tiled=True).reshape(size * shard.shape[0], shard.shape[1])


def exchange(value):
    size = lax.axis_size(GRID)
    parts = value.reshape(size, value.shape[0] // size, value.shape[1])
    return lax.all_to_all(parts, GRID, 0, 0, tiled=True)


def on_device(
    tokens,
    attn_in,
    attn_out,
    mlp_in,
    mlp_out,
    norm_gain,
    norm_shift,
    head_bias,
    unit_bias,
    branch_bias,
    cotangent,
):
    _, rows, width = tokens.shape
    layers, shard, _, local_w = attn_in.shape
    local_f = mlp_in.shape[2]
    ranks = lax.axis_size("mp")
    rank = lax.axis_index("mp")
    half = lax.axis_index("ctx")
    share = rows // ranks
    share_w = width // ranks

    def rotated(block):
        return lax.dynamic_slice_in_dim(jnp.concatenate([block, block], axis=0), rank * share, rows, 0)

    def restored(block):
        start = rows - rank * share
        return lax.dynamic_slice_in_dim(jnp.concatenate([block, block], axis=0), start, rows, 0)

    place = (jnp.arange(rows) + rank * share) % rows
    mask = jnp.where(place[:, None] <= place[None, :], 0.0, -1e30).astype(F32)
    half = half.reshape(1)

    flat_in = attn_in.reshape(layers, shard, 3 * local_w)
    first = spread(jnp.concatenate([flat_in[0], attn_out[0]], axis=1))
    packed = jnp.concatenate([mlp_in[0], mlp_out[0]], axis=1)
    near = lax.all_gather(packed, GRID, axis=0, tiled=True)
    packed = jnp.concatenate([flat_in[1], attn_out[1], mlp_in[1], mlp_out[1]], axis=1)
    rest = lax.all_gather(packed, GRID, axis=0, tiled=True)
    w3, w4 = 3 * local_w, 4 * local_w
    weights = [
        (first[:, :w3], first[:, w3:], near[:, :local_f], near[:, local_f:]),
        (rest[:, :w3], rest[:, w3:w4], rest[:, w4 : w4 + local_f], rest[:, w4 + local_f :]),
    ]

    low_tokens = rotated(tokens.reshape(rows, width))
    state = low_tokens[:share].astype(F32)
    saved = []
    for layer in range(layers):
        w_in, w_out, w_up, w_down = weights[layer]
        if layer == 0:
            normed, scaled_all, inv_all = normalize_fwd(
                low_tokens.astype(F32), norm_gain[layer, 0], norm_shift[layer, 0]
            )
            a_low, a_scaled, a_inv = normed.astype(BF), scaled_all[:share], inv_all[:share]
            first_scaled = scaled_all
        else:
            normed, a_scaled, a_inv = normalize_fwd(state, norm_gain[layer, 0], norm_shift[layer, 0])
            a_low = gather_rows(normed.astype(BF))
        projected = matmul(a_low, w_in)
        query = (projected[:, :local_w] + head_bias[layer, 0]).astype(BF)
        keys = projected[:, local_w : 2 * local_w].astype(BF)
        values = (projected[:, 2 * local_w :] + head_bias[layer, 1]).astype(BF)
        own = jnp.stack([keys, values])
        far = swap(own)
        heads_low, logsum = attend_forward(half, mask, query, own, far)
        middle = state + scatter_rows(matmul_t(heads_low, w_out)) + branch_bias[layer, 0]
        second, c_scaled, c_inv = normalize_fwd(middle, norm_gain[layer, 1], norm_shift[layer, 1])
        c_low = gather_blocks(second.astype(BF))
        hidden = [matmul(block, w_up) + unit_bias[layer] for block in c_low]
        active = [jax.nn.gelu(block, approximate=True).astype(BF) for block in hidden]
        if layer < layers - 1:
            parts = [matmul_t(block, w_down) for block in active]
            state = middle + return_blocks(parts) + branch_bias[layer, 1]
        saved.append(
            (a_low, a_scaled, a_inv, query, own, far, logsum, heads_low)
            + (c_low, c_scaled, c_inv, hidden, active)
        )
    grad_low = rotated(cotangent.reshape(rows, width))
    grad_low = row_blocks(grad_low)
    grad = grad_low[0].astype(F32)
    gains, shifts, heads_b, units_b, branches_b, matrices = {}, {}, {}, {}, {}, {}
    size = lax.axis_size(GRID)
    attn_pairs = []
    for layer in reversed(range(layers)):
        w_in, w_out, w_up, w_down = weights[layer]
        a_low, a_scaled, a_inv, query, own, far, logsum, heads_low = saved[layer][:8]
        c_low, c_scaled, c_inv, hidden, active = saved[layer][8:]
        if layer < layers - 1:
            grad_low = gather_blocks(grad.astype(BF))
        bias_down = jnp.sum(grad, axis=0)
        d_hidden = []
        for block, low in zip(hidden, grad_low, strict=True):
            gelu_pull = jax.vjp(partial(jax.nn.gelu, approximate=True), block)[1]
            d_hidden.append(gelu_pull(matmul(low, w_down))[0])
        units_b[layer] = sum(jnp.sum(block, axis=0) for block in d_hidden)
        hidden_low = [block.astype(BF) for block in d_hidden]
        parts = [matmul_t(block, w_up) for block in hidden_low]
        products = weight_products(attn_pairs + [(c_low, hidden_low), (grad_low, active)])
        d_second, products = return_blocks(parts, products)
        matrices[layer] = products
        d_middle, gain_two, shift_two = normalize_back(d_second, c_scaled, c_inv, norm_gain[layer, 1])
        grad_mid = grad + d_middle
        bias_attn = jnp.sum(grad_mid, axis=0)
        branches_b[layer] = jnp.stack([bias_attn, bias_down])
        if layer == layers - 1:
            mid_low = gather_rows(grad_mid.astype(BF))
        else:
            shared = [gains[1], shifts[1], gain_two[None], shift_two[None], branches_b[0], branches_b[1]]
            shared = jnp.pad(jnp.concatenate(shared), ((0, 6), (0, 0))).astype(BF)
            blocks = gather_blocks(jnp.concatenate([grad_mid.astype(BF), shared], axis=0))
            mid_low = jnp.concatenate([block[:share] for block in blocks], axis=0)
            lines = by_rank([block[share : share + 10] for block in blocks])
            shared = jnp.sum(lines.astype(F32), axis=0).reshape(10, ranks, share_w)
            shared = lax.dynamic_index_in_dim(shared, rank, 1, False).reshape(-1)
        d_heads = matmul(mid_low, w_out).astype(BF)
        if layer == layers - 1:
            d_heads, active = lax.optimization_barrier((d_heads, active))
            parts = [matmul_t(block, w_down) for block in active]
            state = middle + return_blocks(parts) + branch_bias[layer, 1]
        else:
            d_heads, state_low = lax.optimization_barrier((d_heads, state.astype(BF)))
            mixed = restored(gather_rows(state_low))
        d_query, d_own, d_far = attend_backward(half, mask, query, own, far, d_heads, logsum)
        d_own = d_own + swap(d_far).astype(F32)
        heads_b[layer] = jnp.stack([jnp.sum(d_query, axis=0), jnp.sum(d_own[1], axis=0)])
        d_projected = jnp.concatenate([d_query, d_own[0], d_own[1]], axis=1).astype(BF)
        d_partial = matmul_t(d_projected, w_in)
        if layer == layers - 1:
            attn_pairs = [(a_low, d_projected), (mid_low, heads_low)]
        else:
            line = [jnp.sum(d_partial * first_scaled, axis=0), jnp.sum(d_partial, axis=0), shared]
            line += [heads_b[0].reshape(-1), heads_b[1].reshape(-1), units_b[0], units_b[1]]
            line = jnp.concatenate(line)
            line = jnp.pad(line, (0, shard * 256 - line.shape[0])).astype(BF).reshape(shard, 256)
            line = jnp.broadcast_to(line[None], (size, shard, 256)).reshape(size * shard, 256)
            pairs = [(a_low, d_projected), (mid_low, heads_low)]
            moved = jnp.sum(exchange(weight_products(pairs, line)).astype(F32), axis=0)
            grad_in_first, grad_out_first = moved[:, :w3], moved[:, w3:w4]
            line = moved[:, w4:].reshape(-1)
        d_normed = scatter_rows(d_partial)
        d_state, gain_one, shift_one = normalize_back(d_normed, a_scaled, a_inv, norm_gain[layer, 0])
        grad = grad_mid + d_state
        gains[layer] = jnp.stack([gain_one, gain_two])
        shifts[layer] = jnp.stack([shift_one, shift_two])

    def reduced(packed):
        return lax.psum_scatter(packed, GRID, scatter_dimension=0, tiled=True).astype(F32)

    early, later = reduced(matrices[1]), reduced(matrices[0])
    all_in = jnp.stack([grad_in_first, later[:, :w3]]).reshape(layers, shard, 3, local_w)
    all_out = jnp.stack([grad_out_first, later[:, w3:w4]])
    all_up = jnp.stack([later[:, w4 : w4 + local_f], early[:, :local_f]])
    all_down = jnp.stack([later[:, w4 + local_f :], early[:, local_f:]])

    token_grad = restored(gather_rows(grad.astype(BF))).astype(F32)
    cut = 2 * width + 10 * share_w
    lines = by_rank(gather_blocks(line[:cut].reshape(-1, share_w)))
    late = jnp.sum(lines[:, : 2 * ranks], axis=0).reshape(2, width)
    shared = lines[:, 2 * ranks :].transpose(1, 0, 2).reshape(10, width)
    gain_grad = jnp.stack([late[0], shared[4], shared[0], shared[1]]).reshape(layers, 2, width)
    shift_grad = jnp.stack([late[1], shared[5], shared[2], shared[3]]).reshape(layers, 2, width)
    branch_grad = shared[6:10].reshape(layers, 2, width)
    head_grad = line[cut : cut + layers * 2 * local_w].reshape(layers, 2, local_w)
    cut += layers * 2 * local_w
    unit_grad = line[cut : cut + layers * local_f].reshape(layers, local_f)
    return (
        mixed.reshape(1, rows, width),
        token_grad.reshape(1, rows, width),
        all_in,
        all_out,
        all_up,
        all_down,
        gain_grad,
        shift_grad,
        head_grad,
        unit_grad,
        branch_grad,
    )


def solution(mesh):
    return jax.shard_map(
        on_device,
        mesh=mesh,
        in_specs=(
            P("dp", "ctx", None),
            P(None, ("dp", "ctx"), None, "mp"),
            P(None, ("dp", "ctx"), "mp"),
            P(None, ("dp", "ctx"), "mp"),
            P(None, ("dp", "ctx"), "mp"),
            P(),
            P(),
            P(None, None, "mp"),
            P(None, "mp"),
            P(),
            P("dp", "ctx", None),
        ),
        out_specs=(
            P("dp", "ctx", None),
            P("dp", "ctx", None),
            P(None, ("dp", "ctx"), None, "mp"),
            P(None, ("dp", "ctx"), "mp"),
            P(None, ("dp", "ctx"), "mp"),
            P(None, ("dp", "ctx"), "mp"),
            P(),
            P(),
            P(None, None, "mp"),
            P(None, "mp"),
            P(),
        ),
        check_vma=False,
    )
```

```python
from functools import partial

import jax
import jax.numpy as jnp
from jax import lax
from jax.experimental import pallas as pl
from jax.experimental.pallas import tpu as pltpu
from jax.sharding import PartitionSpec as P

HEAD_DIM = 64
EPS = 1e-05
BF = jnp.bfloat16
F32 = jnp.float32
GRID = ("dp", "ctx")
LOG2E = 1.4426950408889634


def matmul(left, right):
    return jnp.dot(left, right, preferred_element_type=F32)


def matmul_t(left, right):
    return lax.dot_general(left, right, (((1,), (1,)), ((), ())), preferred_element_type=F32)


def matmul_tn(left, right):
    return lax.dot_general(left, right, (((0,), (0,)), ((), ())), preferred_element_type=F32)


def normalize_fwd(value, gain, shift):
    mean = jnp.mean(value, axis=-1, keepdims=True)
    centred = value - mean
    variance = jnp.mean(centred * centred, axis=-1, keepdims=True)
    inverse = lax.rsqrt(variance + EPS)
    scaled = centred * inverse
    return (scaled * gain + shift, scaled, inverse)


def normalize_back(grad, scaled, inverse, gain):
    weighted = grad * gain
    first = jnp.mean(weighted, axis=-1, keepdims=True)
    second = jnp.mean(weighted * scaled, axis=-1, keepdims=True)
    return (
        inverse * (weighted - first - scaled * second),
        jnp.sum(grad * scaled, axis=0),
        jnp.sum(grad, axis=0),
    )


def head_lanes(block, head):
    lane = lax.broadcasted_iota(jnp.int32, block.shape, 1)
    return jnp.where((lane >= HEAD_DIM) == (head == 1), block, jnp.zeros_like(block))


def attend_kernel(half_ref, mask_ref, q_ref, own_ref, far_ref, o_ref, lse_ref):
    factor = HEAD_DIM ** (-0.5) * LOG2E

    def run(far):
        out = None
        for head in range(2):
            query = head_lanes(q_ref[...], head)
            near_s = matmul_t(own_ref[0], query) * factor + mask_ref[...]
            top = jnp.max(near_s, axis=0, keepdims=True)
            if far:
                far_s = matmul_t(far_ref[0], query) * factor
                top = jnp.maximum(top, jnp.max(far_s, axis=0, keepdims=True))
            near_p = jnp.exp2(near_s - top)
            total = jnp.sum(near_p, axis=0, keepdims=True)
            mixed = matmul_tn(head_lanes(own_ref[1], head), near_p.astype(BF))
            if far:
                far_p = jnp.exp2(far_s - top)
                total = total + jnp.sum(far_p, axis=0, keepdims=True)
                mixed = mixed + matmul_tn(head_lanes(far_ref[1], head), far_p.astype(BF))
            lse_ref[0, head : head + 1, :] = top + jnp.log2(total)
            mixed = mixed / total
            out = mixed if out is None else out + mixed
        o_ref[...] = out.T.astype(BF)

    pl.when(half_ref[0] == 1)(lambda: run(True))
    pl.when(half_ref[0] == 0)(lambda: run(False))


def attend_back_kernel(
    half_ref, mask_ref, q_ref, own_ref, far_ref, g_ref, lse_ref, dq_ref, down_ref, dfar_ref
):
    scale = HEAD_DIM ** (-0.5)
    factor = scale * LOG2E

    def run(far):
        refs = [own_ref] + ([far_ref] if far else [])
        d_query, d_keys, d_values = None, [None, None], [None, None]
        for head in range(2):
            query, grad = head_lanes(q_ref[...], head), head_lanes(g_ref[...], head)
            lse = lse_ref[0, head : head + 1, :]
            weights, d_weights, inner = [], [], None
            for index, ref in enumerate(refs):
                scores = matmul_t(ref[0], query) * factor - lse
                if index == 0:
                    scores = scores + mask_ref[...]
                weights.append(jnp.exp2(scores))
                d_weights.append(matmul_t(ref[1], grad))
                part = jnp.sum(weights[-1] * d_weights[-1], axis=0, keepdims=True)
                inner = part if inner is None else inner + part
            for index, ref in enumerate(refs):
                d_scores = (weights[index] * (d_weights[index] - inner)).astype(BF)
                part_k = matmul(d_scores, query)
                part_v = matmul(weights[index].astype(BF), grad)
                part_q = matmul_tn(head_lanes(ref[0], head), d_scores)
                d_keys[index] = part_k if d_keys[index] is None else d_keys[index] + part_k
                d_values[index] = part_v if d_values[index] is None else d_values[index] + part_v
                d_query = part_q if d_query is None else d_query + part_q
        dq_ref[...] = d_query.T * scale
        down_ref[0] = d_keys[0] * scale
        down_ref[1] = d_values[0]
        if far:
            dfar_ref[0] = (d_keys[1] * scale).astype(BF)
            dfar_ref[1] = d_values[1].astype(BF)
        else:
            dfar_ref[...] = jnp.zeros(dfar_ref.shape, BF)

    pl.when(half_ref[0] == 1)(lambda: run(True))
    pl.when(half_ref[0] == 0)(lambda: run(False))


def attend_specs(rows):
    pair = 2 * HEAD_DIM
    return (
        pl.BlockSpec(memory_space=pltpu.SMEM),
        pl.BlockSpec((rows, rows), lambda i: (0, 0)),
        pl.BlockSpec((rows, pair), lambda i: (0, i)),
        pl.BlockSpec((2, rows, pair), lambda i: (0, 0, i)),
        pl.BlockSpec((1, 2, rows), lambda i: (i, 0, 0)),
    )


def kernel_params(flops, moved):
    return dict(
        compiler_params=pltpu.CompilerParams(vmem_limit_bytes=40 * 1024 * 1024),
        cost_estimate=pl.CostEstimate(flops=flops, bytes_accessed=moved, transcendentals=0),
    )


def attend_forward(half, mask, query, own, far):
    rows, width = query.shape
    pairs = width // (2 * HEAD_DIM)
    scalar, square, flat, both, line = attend_specs(rows)
    return pl.pallas_call(
        attend_kernel,
        grid=(pairs,),
        in_specs=[scalar, square, flat, both, both],
        out_specs=[flat, line],
        out_shape=[
            jax.ShapeDtypeStruct((rows, width), BF),
            jax.ShapeDtypeStruct((pairs, 2, rows), F32),
        ],
        **kernel_params(1000000000, 4000000),
    )(half, mask, query, own, far)


def attend_backward(half, mask, query, own, far, grad, lse):
    rows, width = query.shape
    pairs = width // (2 * HEAD_DIM)
    scalar, square, flat, both, line = attend_specs(rows)
    return pl.pallas_call(
        attend_back_kernel,
        grid=(pairs,),
        in_specs=[scalar, square, flat, both, both, flat, line],
        out_specs=[flat, both, both],
        out_shape=[
            jax.ShapeDtypeStruct((rows, width), F32),
            jax.ShapeDtypeStruct((2, rows, width), F32),
            jax.ShapeDtypeStruct((2, rows, width), BF),
        ],
        **kernel_params(1000000000, 6000000),
    )(half, mask, query, own, far, grad, lse)


def product_kernel(counts, *refs):
    out_ref, at, column = refs[-1], 0, 0

    def taken(count):
        nonlocal at
        blocks = [ref[...] for ref in refs[at : at + count]]
        at += count
        return blocks[0] if count == 1 else jnp.concatenate(blocks, axis=0)

    for left_count, right_count in counts:
        left, right = taken(left_count), taken(right_count)
        width = right.shape[1]
        out_ref[:, column : column + width] = matmul_tn(left, right).astype(BF)
        column += width
    if at < len(refs) - 1:
        out_ref[:, column:] = refs[at][...]


def weight_products(pairs, extra=None):
    pairs = [[x if isinstance(x, list) else [x] for x in pair] for pair in pairs]
    height = pairs[0][0][0].shape[1]
    tile = 256
    specs, operands, width = [], [], 0
    for left, right in pairs:
        specs += [pl.BlockSpec((x.shape[0], tile), lambda i: (0, i)) for x in left]
        specs += [pl.BlockSpec(x.shape, lambda i: (0, 0)) for x in right]
        operands += [*left, *right]
        width += right[0].shape[1]
    if extra is not None:
        specs.append(pl.BlockSpec((tile, extra.shape[1]), lambda i: (i, 0)))
        operands.append(extra)
        width += extra.shape[1]
    return pl.pallas_call(
        partial(product_kernel, [(len(left), len(right)) for left, right in pairs]),
        grid=(height // tile,),
        in_specs=specs,
        out_specs=pl.BlockSpec((tile, width), lambda i: (i, 0)),
        out_shape=pltpu.HBM((height, width), BF),
        **kernel_params(1000000, 1000000),
    )(*operands)


def shifted(size, step):
    return [(i, (i + step) % size) for i in range(size)]


def gather_blocks(own):
    size = lax.axis_size("mp")
    return [own] + [lax.ppermute(own, "mp", shifted(size, -step)) for step in range(1, size)]


def gather_rows(own):
    return jnp.concatenate(gather_blocks(own), axis=0)


def return_blocks(blocks, beside=None):
    size = lax.axis_size("mp")
    parts = [
        lax.ppermute(blocks[step].astype(BF), "mp", shifted(size, step)) for step in range(1, size)
    ]
    if beside is not None:
        parts[1], beside = lax.optimization_barrier((parts[1], beside))
    total = blocks[0]
    for part in parts:
        total = total + part.astype(F32)
    return total if beside is None else (total, beside)


def restore_kernel(rank_ref, *refs):
    for step in range(len(refs) - 1):

        @pl.when(pl.program_id(0) == step)
        def _(step=step):
            refs[-1][...] = refs[step][...].astype(refs[-1].dtype)


def restored(blocks, rank, kind):
    count = len(blocks)
    share, width = blocks[0].shape
    return pl.pallas_call(
        restore_kernel,
        grid_spec=pltpu.PrefetchScalarGridSpec(
            num_scalar_prefetch=1,
            grid=(count,),
            in_specs=[pl.BlockSpec((share, width), lambda i, rank_ref: (0, 0))] * count,
            out_specs=pl.BlockSpec(
                (share, width), lambda i, rank_ref: (lax.rem(i + rank_ref[0], count), 0)
            ),
        ),
        out_shape=jax.ShapeDtypeStruct((count * share, width), kind),
        **kernel_params(1000000, 1000000),
    )(rank, *blocks)


def by_rank(blocks):
    size = lax.axis_size("mp")
    start = lax.rem(size - lax.axis_index("mp"), size)
    return lax.dynamic_slice_in_dim(jnp.stack(blocks + blocks), start, size, 0)


def row_blocks(value):
    share = value.shape[0] // lax.axis_size("mp")
    return [value[at : at + share] for at in range(0, value.shape[0], share)]


def scatter_rows(partial_sum):
    return return_blocks(row_blocks(partial_sum))


def swap(value):
    return lax.ppermute(value, "ctx", [(0, 1), (1, 0)])


def spread(shard):
    size = lax.axis_size(GRID)
    copies = jnp.broadcast_to(shard[None], (size, *shard.shape))
    return lax.all_to_all(copies, GRID, 0, 0, tiled=True).reshape(size * shard.shape[0], shard.shape[1])


def exchange(value):
    size = lax.axis_size(GRID)
    parts = value.reshape(size, value.shape[0] // size, value.shape[1])
    return lax.all_to_all(parts, GRID, 0, 0, tiled=True)


def on_device(
    tokens,
    attn_in,
    attn_out,
    mlp_in,
    mlp_out,
    norm_gain,
    norm_shift,
    head_bias,
    unit_bias,
    branch_bias,
    cotangent,
):
    _, rows, width = tokens.shape
    layers, shard, _, local_w = attn_in.shape
    local_f = mlp_in.shape[2]
    ranks = lax.axis_size("mp")
    rank = lax.axis_index("mp")
    half = lax.axis_index("ctx")
    share = rows // ranks
    share_w = width // ranks

    def rotated(block):
        return lax.dynamic_slice_in_dim(jnp.concatenate([block, block], axis=0), rank * share, rows, 0)

    place = (jnp.arange(rows) + rank * share) % rows
    mask = jnp.where(place[:, None] <= place[None, :], 0.0, -1e30).astype(F32)
    half = half.reshape(1)
    ranks_at = rank.reshape(1)

    flat_in = attn_in.reshape(layers, shard, 3 * local_w)
    first = spread(jnp.concatenate([flat_in[0], attn_out[0]], axis=1))
    packed = jnp.concatenate([mlp_in[0], mlp_out[0]], axis=1)
    near = lax.all_gather(packed, GRID, axis=0, tiled=True)
    packed = jnp.concatenate([flat_in[1], attn_out[1], mlp_in[1], mlp_out[1]], axis=1)
    rest = lax.all_gather(packed, GRID, axis=0, tiled=True)
    w3, w4 = 3 * local_w, 4 * local_w
    weights = [
        (first[:, :w3], first[:, w3:], near[:, :local_f], near[:, local_f:]),
        (rest[:, :w3], rest[:, w3:w4], rest[:, w4 : w4 + local_f], rest[:, w4 + local_f :]),
    ]

    low_tokens = rotated(tokens.reshape(rows, width))
    state = low_tokens[:share].astype(F32)
    saved = []
    for layer in range(layers):
        w_in, w_out, w_up, w_down = weights[layer]
        if layer == 0:
            normed, scaled_all, inv_all = normalize_fwd(
                low_tokens.astype(F32), norm_gain[layer, 0], norm_shift[layer, 0]
            )
            a_low, a_scaled, a_inv = normed.astype(BF), scaled_all[:share], inv_all[:share]
            first_scaled = scaled_all
        else:
            normed, a_scaled, a_inv = normalize_fwd(state, norm_gain[layer, 0], norm_shift[layer, 0])
            a_low = gather_rows(normed.astype(BF))
        projected = matmul(a_low, w_in)
        query = (projected[:, :local_w] + head_bias[layer, 0]).astype(BF)
        keys = projected[:, local_w : 2 * local_w].astype(BF)
        values = (projected[:, 2 * local_w :] + head_bias[layer, 1]).astype(BF)
        own = jnp.stack([keys, values])
        far = swap(own)
        heads_low, logsum = attend_forward(half, mask, query, own, far)
        middle = state + scatter_rows(matmul_t(heads_low, w_out)) + branch_bias[layer, 0]
        second, c_scaled, c_inv = normalize_fwd(middle, norm_gain[layer, 1], norm_shift[layer, 1])
        c_low = gather_blocks(second.astype(BF))
        hidden = [matmul(block, w_up) + unit_bias[layer] for block in c_low]
        active = [jax.nn.gelu(block, approximate=True).astype(BF) for block in hidden]
        if layer < layers - 1:
            parts = [matmul_t(block, w_down) for block in active]
            state = middle + return_blocks(parts) + branch_bias[layer, 1]
        saved.append(
            (a_low, a_scaled, a_inv, query, own, far, logsum, heads_low)
            + (c_low, c_scaled, c_inv, hidden, active)
        )
    grad_low = rotated(cotangent.reshape(rows, width))
    grad_low = row_blocks(grad_low)
    grad = grad_low[0].astype(F32)
    gains, shifts, heads_b, units_b, branches_b, matrices = {}, {}, {}, {}, {}, {}
    def reduced(packed):
        return lax.psum_scatter(packed, GRID, scatter_dimension=0, tiled=True).astype(F32)

    size = lax.axis_size(GRID)
    attn_pairs = []
    for layer in reversed(range(layers)):
        w_in, w_out, w_up, w_down = weights[layer]
        a_low, a_scaled, a_inv, query, own, far, logsum, heads_low = saved[layer][:8]
        c_low, c_scaled, c_inv, hidden, active = saved[layer][8:]
        if layer < layers - 1:
            grad_low = gather_blocks(grad.astype(BF))
        bias_down = jnp.sum(grad, axis=0)
        d_hidden = []
        for block, low in zip(hidden, grad_low, strict=True):
            gelu_pull = jax.vjp(partial(jax.nn.gelu, approximate=True), block)[1]
            d_hidden.append(gelu_pull(matmul(low, w_down))[0])
        units_b[layer] = sum(jnp.sum(block, axis=0) for block in d_hidden)
        hidden_low = [block.astype(BF) for block in d_hidden]
        parts = [matmul_t(block, w_up) for block in hidden_low]
        products = weight_products(attn_pairs + [(c_low, hidden_low), (grad_low, active)])
        if layer == layers - 1:
            d_second, products = return_blocks(parts, products)
        else:
            d_second, (products, early) = return_blocks(parts, (products, reduced(matrices[1])))
        matrices[layer] = products
        d_middle, gain_two, shift_two = normalize_back(d_second, c_scaled, c_inv, norm_gain[layer, 1])
        grad_mid = grad + d_middle
        bias_attn = jnp.sum(grad_mid, axis=0)
        branches_b[layer] = jnp.stack([bias_attn, bias_down])
        if layer == layers - 1:
            mid_own, active[0] = lax.optimization_barrier((grad_mid.astype(BF), active[0]))
            parts = row_blocks(matmul_t(jnp.concatenate(active, axis=0), w_down))
            parts = parts[:1] + [part.astype(BF) for part in parts[1:]]
            mid_low = gather_rows(mid_own)
        else:
            shared = [gains[1], shifts[1], gain_two[None], shift_two[None], branches_b[0], branches_b[1]]
            shared = jnp.pad(jnp.concatenate(shared), ((0, 6), (0, 0))).astype(BF)
            blocks = gather_blocks(jnp.concatenate([grad_mid.astype(BF), shared], axis=0))
            mid_low = jnp.concatenate([block[:share] for block in blocks], axis=0)
            lines = by_rank([block[share : share + 10] for block in blocks])
            shared = jnp.sum(lines.astype(F32), axis=0).reshape(10, ranks, share_w)
            shared = lax.dynamic_index_in_dim(shared, rank, 1, False).reshape(-1)
        d_heads = matmul(mid_low, w_out).astype(BF)
        if layer == layers - 1:
            d_heads, parts = lax.optimization_barrier((d_heads, parts))
            state = middle + return_blocks(parts) + branch_bias[layer, 1]
        else:
            d_heads, state_low = lax.optimization_barrier((d_heads, state_low))
            mixed = gather_blocks(state_low)
        d_query, d_own, d_far = attend_backward(half, mask, query, own, far, d_heads, logsum)
        if layer == layers - 1:
            d_query, state_low = lax.optimization_barrier((d_query, state.astype(BF)))
        else:
            d_query, mixed = lax.optimization_barrier((d_query, mixed))
            mixed = restored(mixed, ranks_at, BF)
        d_own = d_own + swap(d_far).astype(F32)
        heads_b[layer] = jnp.stack([jnp.sum(d_query, axis=0), jnp.sum(d_own[1], axis=0)])
        d_projected = jnp.concatenate([d_query, d_own[0], d_own[1]], axis=1).astype(BF)
        d_partial = matmul_t(d_projected, w_in)
        if layer == layers - 1:
            attn_pairs = [(a_low, d_projected), (mid_low, heads_low)]
        else:
            line = [jnp.sum(d_partial * first_scaled, axis=0), jnp.sum(d_partial, axis=0), shared]
            line += [heads_b[0].reshape(-1), heads_b[1].reshape(-1), units_b[0], units_b[1]]
            line = jnp.concatenate(line)
            line = jnp.pad(line, (0, shard * 256 - line.shape[0])).astype(BF).reshape(shard, 256)
            line = jnp.broadcast_to(line[None], (size, shard, 256)).reshape(size * shard, 256)
            pairs = [(a_low, d_projected), (mid_low, heads_low)]
            line, d_partial = lax.optimization_barrier((weight_products(pairs, line), d_partial))
            moved = jnp.sum(exchange(line).astype(F32), axis=0)
            grad_in_first, grad_out_first = moved[:, :w3], moved[:, w3:w4]
            line = moved[:, w4:].reshape(-1)
        d_normed = scatter_rows(d_partial)
        d_state, gain_one, shift_one = normalize_back(d_normed, a_scaled, a_inv, norm_gain[layer, 0])
        grad = grad_mid + d_state
        gains[layer] = jnp.stack([gain_one, gain_two])
        shifts[layer] = jnp.stack([shift_one, shift_two])

    later = reduced(matrices[0])
    all_in = jnp.stack([grad_in_first, later[:, :w3]]).reshape(layers, shard, 3, local_w)
    all_out = jnp.stack([grad_out_first, later[:, w3:w4]])
    all_up = jnp.stack([later[:, w4 : w4 + local_f], early[:, :local_f]])
    all_down = jnp.stack([later[:, w4 + local_f :], early[:, local_f:]])

    token_grad = restored(gather_blocks(grad.astype(BF)), ranks_at, F32)
    cut = 2 * width + 10 * share_w
    lines = by_rank(gather_blocks(line[:cut].reshape(-1, share_w)))
    late = jnp.sum(lines[:, : 2 * ranks], axis=0).reshape(2, width)
    shared = lines[:, 2 * ranks :].transpose(1, 0, 2).reshape(10, width)
    gain_grad = jnp.stack([late[0], shared[4], shared[0], shared[1]]).reshape(layers, 2, width)
    shift_grad = jnp.stack([late[1], shared[5], shared[2], shared[3]]).reshape(layers, 2, width)
    branch_grad = shared[6:10].reshape(layers, 2, width)
    head_grad = line[cut : cut + layers * 2 * local_w].reshape(layers, 2, local_w)
    cut += layers * 2 * local_w
    unit_grad = line[cut : cut + layers * local_f].reshape(layers, local_f)
    return (
        mixed.reshape(1, rows, width),
        token_grad.reshape(1, rows, width),
        all_in,
        all_out,
        all_up,
        all_down,
        gain_grad,
        shift_grad,
        head_grad,
        unit_grad,
        branch_grad,
    )


def solution(mesh):
    return jax.shard_map(
        on_device,
        mesh=mesh,
        in_specs=(
            P("dp", "ctx", None),
            P(None, ("dp", "ctx"), None, "mp"),
            P(None, ("dp", "ctx"), "mp"),
            P(None, ("dp", "ctx"), "mp"),
            P(None, ("dp", "ctx"), "mp"),
            P(),
            P(),
            P(None, None, "mp"),
            P(None, "mp"),
            P(),
            P("dp", "ctx", None),
        ),
        out_specs=(
            P("dp", "ctx", None),
            P("dp", "ctx", None),
            P(None, ("dp", "ctx"), None, "mp"),
            P(None, ("dp", "ctx"), "mp"),
            P(None, ("dp", "ctx"), "mp"),
            P(None, ("dp", "ctx"), "mp"),
            P(),
            P(),
            P(None, None, "mp"),
            P(None, "mp"),
            P(),
        ),
        check_vma=False,
    )
```

```python
from functools import partial

import jax
import jax.numpy as jnp
from jax import lax
from jax.experimental import pallas as pl
from jax.experimental.pallas import tpu as pltpu
from jax.sharding import PartitionSpec as P

HEAD_DIM = 64
EPS = 1e-05
BF = jnp.bfloat16
F32 = jnp.float32
GRID = ("dp", "ctx")
CHUNK = 32
LOG2E = 1.4426950408889634


def matmul(left, right):
    return jnp.dot(left, right, preferred_element_type=F32)


def matmul_t(left, right):
    return lax.dot_general(left, right, (((1,), (1,)), ((), ())), preferred_element_type=F32)


def matmul_tn(left, right):
    return lax.dot_general(left, right, (((0,), (0,)), ((), ())), preferred_element_type=F32)


def normalize_fwd(value, gain, shift):
    mean = jnp.mean(value, axis=-1, keepdims=True)
    centred = value - mean
    variance = jnp.mean(centred * centred, axis=-1, keepdims=True)
    inverse = lax.rsqrt(variance + EPS)
    scaled = centred * inverse
    return (scaled * gain + shift, scaled, inverse)


def normalize_back(grad, scaled, inverse, gain):
    weighted = grad * gain
    first = jnp.mean(weighted, axis=-1, keepdims=True)
    second = jnp.mean(weighted * scaled, axis=-1, keepdims=True)
    return (
        inverse * (weighted - first - scaled * second),
        jnp.sum(grad * scaled, axis=0),
        jnp.sum(grad, axis=0),
    )


def head_lanes(block, head):
    lane = lax.broadcasted_iota(jnp.int32, block.shape, 1)
    return jnp.where((lane >= HEAD_DIM) == (head == 1), block, jnp.zeros_like(block))


def attend_kernel(half_ref, mask_ref, q_ref, own_ref, far_ref, o_ref, lse_ref):
    factor = HEAD_DIM ** (-0.5) * LOG2E

    def run(far):
        out = None
        for head in range(2):
            query = head_lanes(q_ref[...], head)
            near_s = matmul_t(own_ref[0], query) * factor + mask_ref[...]
            top = jnp.max(near_s, axis=0, keepdims=True)
            if far:
                far_s = matmul_t(far_ref[0], query) * factor
                top = jnp.maximum(top, jnp.max(far_s, axis=0, keepdims=True))
            near_p = jnp.exp2(near_s - top)
            total = jnp.sum(near_p, axis=0, keepdims=True)
            mixed = matmul_tn(head_lanes(own_ref[1], head), near_p.astype(BF))
            if far:
                far_p = jnp.exp2(far_s - top)
                total = total + jnp.sum(far_p, axis=0, keepdims=True)
                mixed = mixed + matmul_tn(head_lanes(far_ref[1], head), far_p.astype(BF))
            lse_ref[0, head : head + 1, :] = top + jnp.log2(total)
            mixed = mixed / total
            out = mixed if out is None else out + mixed
        o_ref[...] = out.T.astype(BF)

    pl.when(half_ref[0] == 1)(lambda: run(True))
    pl.when(half_ref[0] == 0)(lambda: run(False))


def attend_back_kernel(
    half_ref, mask_ref, q_ref, own_ref, far_ref, g_ref, lse_ref, dq_ref, down_ref, dfar_ref
):
    scale = HEAD_DIM ** (-0.5)
    factor = scale * LOG2E

    def run(far):
        refs = [own_ref] + ([far_ref] if far else [])
        d_query, d_keys, d_values = None, [None, None], [None, None]
        for head in range(2):
            query, grad = head_lanes(q_ref[...], head), head_lanes(g_ref[...], head)
            lse = lse_ref[0, head : head + 1, :]
            weights, d_weights, inner = [], [], None
            for index, ref in enumerate(refs):
                scores = matmul_t(ref[0], query) * factor - lse
                if index == 0:
                    scores = scores + mask_ref[...]
                weights.append(jnp.exp2(scores))
                d_weights.append(matmul_t(ref[1], grad))
                part = jnp.sum(weights[-1] * d_weights[-1], axis=0, keepdims=True)
                inner = part if inner is None else inner + part
            for index, ref in enumerate(refs):
                d_scores = (weights[index] * (d_weights[index] - inner)).astype(BF)
                part_k = matmul(d_scores, query)
                part_v = matmul(weights[index].astype(BF), grad)
                part_q = matmul_tn(head_lanes(ref[0], head), d_scores)
                d_keys[index] = part_k if d_keys[index] is None else d_keys[index] + part_k
                d_values[index] = part_v if d_values[index] is None else d_values[index] + part_v
                d_query = part_q if d_query is None else d_query + part_q
        dq_ref[...] = d_query.T * scale
        down_ref[0] = d_keys[0] * scale
        down_ref[1] = d_values[0]
        if far:
            dfar_ref[0] = (d_keys[1] * scale).astype(BF)
            dfar_ref[1] = d_values[1].astype(BF)
        else:
            dfar_ref[...] = jnp.zeros(dfar_ref.shape, BF)

    pl.when(half_ref[0] == 1)(lambda: run(True))
    pl.when(half_ref[0] == 0)(lambda: run(False))


def attend_specs(rows):
    pair = 2 * HEAD_DIM
    return (
        pl.BlockSpec(memory_space=pltpu.SMEM),
        pl.BlockSpec((rows, rows), lambda i: (0, 0)),
        pl.BlockSpec((rows, pair), lambda i: (0, i)),
        pl.BlockSpec((2, rows, pair), lambda i: (0, 0, i)),
        pl.BlockSpec((1, 2, rows), lambda i: (i, 0, 0)),
    )


def kernel_params(flops, moved):
    return dict(
        compiler_params=pltpu.CompilerParams(vmem_limit_bytes=40 * 1024 * 1024),
        cost_estimate=pl.CostEstimate(flops=flops, bytes_accessed=moved, transcendentals=0),
    )


def attend_forward(half, mask, query, own, far):
    rows, width = query.shape
    pairs = width // (2 * HEAD_DIM)
    scalar, square, flat, both, line = attend_specs(rows)
    return pl.pallas_call(
        attend_kernel,
        grid=(pairs,),
        in_specs=[scalar, square, flat, both, both],
        out_specs=[flat, line],
        out_shape=[
            jax.ShapeDtypeStruct((rows, width), BF),
            jax.ShapeDtypeStruct((pairs, 2, rows), F32),
        ],
        **kernel_params(1000000000, 4000000),
    )(half, mask, query, own, far)


def attend_backward(half, mask, query, own, far, grad, lse):
    rows, width = query.shape
    pairs = width // (2 * HEAD_DIM)
    scalar, square, flat, both, line = attend_specs(rows)
    return pl.pallas_call(
        attend_back_kernel,
        grid=(pairs,),
        in_specs=[scalar, square, flat, both, both, flat, line],
        out_specs=[flat, both, both],
        out_shape=[
            jax.ShapeDtypeStruct((rows, width), F32),
            jax.ShapeDtypeStruct((2, rows, width), F32),
            jax.ShapeDtypeStruct((2, rows, width), BF),
        ],
        **kernel_params(1000000000, 6000000),
    )(half, mask, query, own, far, grad, lse)


def product_kernel(counts, *refs):
    out_ref, at, column = refs[-1], 0, 0

    def taken(count):
        nonlocal at
        blocks = [ref[...] for ref in refs[at : at + count]]
        at += count
        return blocks[0] if count == 1 else jnp.concatenate(blocks, axis=0)

    for left_count, right_count in counts:
        left, right = taken(left_count), taken(right_count)
        width = right.shape[1]
        out_ref[:, column : column + width] = matmul_tn(left, right).astype(BF)
        column += width
    if at < len(refs) - 1:
        out_ref[:, column:] = refs[at][...]


def split_kernel(counts, half_ref, *refs):
    tile_ref = refs[-1]
    product_kernel(counts, *refs[:-3], tile_ref)
    tall = tile_ref.shape[0]
    step = CHUNK
    mine, other = refs[-3], refs[-2]
    for at in range(0, tall // 2, step):
        first, second = tile_ref[2 * at : 2 * at + step], tile_ref[2 * at + step : 2 * at + 2 * step]
        low = half_ref[0] == 0
        mine[at : at + step] = jnp.where(low, first, second)
        other[at : at + step] = jnp.where(low, second, first)


def weight_products(pairs, extra=None, half=None):
    pairs = [[x if isinstance(x, list) else [x] for x in pair] for pair in pairs]
    height = pairs[0][0][0].shape[1]
    tile = 256
    specs, operands, width = [], [], 0
    for left, right in pairs:
        specs += [pl.BlockSpec((x.shape[0], tile), lambda i: (0, i)) for x in left]
        specs += [pl.BlockSpec(x.shape, lambda i: (0, 0)) for x in right]
        operands += [*left, *right]
        width += right[0].shape[1]
    if extra is not None:
        specs.append(pl.BlockSpec((tile, extra.shape[1]), lambda i: (i, 0)))
        operands.append(extra)
        width += extra.shape[1]
    if half is not None:
        counts = [(len(left), len(right)) for left, right in pairs]
        return pl.pallas_call(
            partial(split_kernel, counts),
            grid=(height // tile,),
            in_specs=[pl.BlockSpec(memory_space=pltpu.SMEM), *specs],
            out_specs=[pl.BlockSpec((tile // 2, width), lambda i: (i, 0))] * 2,
            out_shape=[pltpu.HBM((height // 2, width), BF)] * 2,
            scratch_shapes=[pltpu.VMEM((tile, width), BF)],
            **kernel_params(1000000, 1000000),
        )(half, *operands)
    return pl.pallas_call(
        partial(product_kernel, [(len(left), len(right)) for left, right in pairs]),
        grid=(height // tile,),
        in_specs=specs,
        out_specs=pl.BlockSpec((tile, width), lambda i: (i, 0)),
        out_shape=pltpu.HBM((height, width), BF),
        **kernel_params(1000000, 1000000),
    )(*operands)


def shifted(size, step):
    return [(i, (i + step) % size) for i in range(size)]


def gather_blocks(own):
    size = lax.axis_size("mp")
    return [own] + [lax.ppermute(own, "mp", shifted(size, -step)) for step in range(1, size)]


def gather_rows(own):
    return jnp.concatenate(gather_blocks(own), axis=0)


def return_blocks(blocks, beside=None):
    size = lax.axis_size("mp")
    parts = [
        lax.ppermute(blocks[step].astype(BF), "mp", shifted(size, step)) for step in range(1, size)
    ]
    if beside is not None:
        parts[1], beside = lax.optimization_barrier((parts[1], beside))
    total = blocks[0]
    for part in parts:
        total = total + part.astype(F32)
    return total if beside is None else (total, beside)


def restore_kernel(rank_ref, *refs):
    for step in range(len(refs) - 1):

        @pl.when(pl.program_id(0) == step)
        def _(step=step):
            refs[-1][...] = refs[step][...].astype(refs[-1].dtype)


def restored(blocks, rank, kind):
    count = len(blocks)
    share, width = blocks[0].shape
    return pl.pallas_call(
        restore_kernel,
        grid_spec=pltpu.PrefetchScalarGridSpec(
            num_scalar_prefetch=1,
            grid=(count,),
            in_specs=[pl.BlockSpec((share, width), lambda i, rank_ref: (0, 0))] * count,
            out_specs=pl.BlockSpec(
                (share, width), lambda i, rank_ref: (lax.rem(i + rank_ref[0], count), 0)
            ),
        ),
        out_shape=jax.ShapeDtypeStruct((count * share, width), kind),
        **kernel_params(1000000, 1000000),
    )(rank, *blocks)


def merged(mine, other):
    return (mine.astype(F32) + swap(other).astype(F32)).astype(BF)


def by_rank(blocks):
    size = lax.axis_size("mp")
    start = lax.rem(size - lax.axis_index("mp"), size)
    return lax.dynamic_slice_in_dim(jnp.stack(blocks + blocks), start, size, 0)


def row_blocks(value):
    share = value.shape[0] // lax.axis_size("mp")
    return [value[at : at + share] for at in range(0, value.shape[0], share)]


def swap(value):
    return lax.ppermute(value, "ctx", [(0, 1), (1, 0)])


def spread(shard):
    size = lax.axis_size(GRID)
    copies = jnp.broadcast_to(shard[None], (size, *shard.shape))
    return lax.all_to_all(copies, GRID, 0, 0, tiled=True).reshape(size * shard.shape[0], shard.shape[1])


def exchange(value, axes):
    size = lax.axis_size(axes)
    parts = value.reshape(size, value.shape[0] // size, value.shape[1])
    return lax.all_to_all(parts, axes, 0, 0, tiled=True)


def on_device(
    tokens,
    attn_in,
    attn_out,
    mlp_in,
    mlp_out,
    norm_gain,
    norm_shift,
    head_bias,
    unit_bias,
    branch_bias,
    cotangent,
):
    _, rows, width = tokens.shape
    layers, shard, _, local_w = attn_in.shape
    local_f = mlp_in.shape[2]
    ranks = lax.axis_size("mp")
    rank = lax.axis_index("mp")
    half = lax.axis_index("ctx")
    share = rows // ranks
    share_w = width // ranks

    def rotated(block):
        return lax.dynamic_slice_in_dim(jnp.concatenate([block, block], axis=0), rank * share, rows, 0)

    place = (jnp.arange(rows) + rank * share) % rows
    mask = jnp.where(place[:, None] <= place[None, :], 0.0, -1e30).astype(F32)
    half = half.reshape(1)
    ranks_at = rank.reshape(1)

    flat_in = attn_in.reshape(layers, shard, 3 * local_w)
    first = spread(jnp.concatenate([flat_in[0], attn_out[0]], axis=1))
    packed = jnp.concatenate([mlp_in[0], mlp_out[0]], axis=1)
    near = lax.all_gather(packed, GRID, axis=0, tiled=True)
    packed = jnp.concatenate([flat_in[1], attn_out[1], mlp_in[1], mlp_out[1]], axis=1)
    rest = lax.all_gather(packed, GRID, axis=0, tiled=True)
    w3, w4 = 3 * local_w, 4 * local_w
    weights = [
        (first[:, :w3], first[:, w3:], near[:, :local_f], near[:, local_f:]),
        (rest[:, :w3], rest[:, w3:w4], rest[:, w4 : w4 + local_f], rest[:, w4 + local_f :]),
    ]

    low_tokens = rotated(tokens.reshape(rows, width))
    state = low_tokens[:share].astype(F32)
    saved = []
    for layer in range(layers):
        w_in, w_out, w_up, w_down = weights[layer]
        if layer == 0:
            normed, scaled_all, inv_all = normalize_fwd(
                low_tokens.astype(F32), norm_gain[layer, 0], norm_shift[layer, 0]
            )
            a_low, a_scaled, a_inv = normed.astype(BF), scaled_all[:share], inv_all[:share]
            first_scaled = scaled_all
        else:
            normed, a_scaled, a_inv = normalize_fwd(state, norm_gain[layer, 0], norm_shift[layer, 0])
            a_low = gather_rows(normed.astype(BF))
        projected = matmul(a_low, w_in)
        query = (projected[:, :local_w] + head_bias[layer, 0]).astype(BF)
        keys = projected[:, local_w : 2 * local_w].astype(BF)
        values = (projected[:, 2 * local_w :] + head_bias[layer, 1]).astype(BF)
        own = jnp.stack([keys, values])
        far = swap(own)
        heads_low, logsum = attend_forward(half, mask, query, own, far)
        parts = [matmul_t(block, w_out) for block in row_blocks(heads_low)]
        middle = state + return_blocks(parts) + branch_bias[layer, 0]
        second, c_scaled, c_inv = normalize_fwd(middle, norm_gain[layer, 1], norm_shift[layer, 1])
        c_low = gather_blocks(second.astype(BF))
        hidden = [matmul(block, w_up) + unit_bias[layer] for block in c_low]
        active = [jax.nn.gelu(block, approximate=True).astype(BF) for block in hidden]
        if layer < layers - 1:
            parts = [matmul_t(block, w_down) for block in active]
            state = middle + return_blocks(parts) + branch_bias[layer, 1]
        saved.append(
            (a_low, a_scaled, a_inv, query, own, far, logsum, heads_low)
            + (c_low, c_scaled, c_inv, hidden, active)
        )
    grad_low = rotated(cotangent.reshape(rows, width))
    grad_low = row_blocks(grad_low)
    grad = grad_low[0].astype(F32)
    gains, shifts, heads_b, units_b, branches_b, matrices = {}, {}, {}, {}, {}, {}
    def reduced(packed):
        return lax.psum_scatter(packed, GRID, scatter_dimension=0, tiled=True)

    size = lax.axis_size(GRID)
    attn_pairs = []
    for layer in reversed(range(layers)):
        w_in, w_out, w_up, w_down = weights[layer]
        a_low, a_scaled, a_inv, query, own, far, logsum, heads_low = saved[layer][:8]
        c_low, c_scaled, c_inv, hidden, active = saved[layer][8:]
        if layer < layers - 1:
            grad_low = gather_blocks(grad.astype(BF))
        bias_down = jnp.sum(grad, axis=0)
        d_hidden = []
        for block, low in zip(hidden, grad_low, strict=True):
            gelu_pull = jax.vjp(partial(jax.nn.gelu, approximate=True), block)[1]
            d_hidden.append(gelu_pull(matmul(low, w_down))[0])
        units_b[layer] = sum(jnp.sum(block, axis=0) for block in d_hidden)
        hidden_low = [block.astype(BF) for block in d_hidden]
        parts = [matmul_t(block, w_up) for block in hidden_low]
        products = weight_products(attn_pairs + [(c_low, hidden_low), (grad_low, active)])
        if layer == layers - 1:
            d_second, products = return_blocks(parts, products)
        else:
            d_second, (products, early) = return_blocks(parts, (products, reduced(matrices[1])))
            early = early.astype(F32)
        matrices[layer] = products
        d_middle, gain_two, shift_two = normalize_back(d_second, c_scaled, c_inv, norm_gain[layer, 1])
        grad_mid = grad + d_middle
        bias_attn = jnp.sum(grad_mid, axis=0)
        branches_b[layer] = jnp.stack([bias_attn, bias_down])
        if layer == layers - 1:
            mid_own, active[0] = lax.optimization_barrier((grad_mid.astype(BF), active[0]))
            parts = row_blocks(matmul_t(jnp.concatenate(active, axis=0), w_down))
            parts = parts[:1] + [part.astype(BF) for part in parts[1:]]
            mid_low = gather_rows(mid_own)
        else:
            shared = [gains[1], shifts[1], gain_two[None], shift_two[None], branches_b[0], branches_b[1]]
            shared = jnp.pad(jnp.concatenate(shared), ((0, 6), (0, 0))).astype(BF)
            blocks = gather_blocks(jnp.concatenate([grad_mid.astype(BF), shared], axis=0))
            mid_low = jnp.concatenate([block[:share] for block in blocks], axis=0)
            shared = sum(block[share : share + 10].astype(F32) for block in blocks)
            shared = shared.reshape(10, ranks, share_w)
            shared = lax.dynamic_index_in_dim(shared, rank, 1, False).reshape(-1)
        d_heads = matmul(mid_low, w_out).astype(BF)
        if layer == layers - 1:
            d_heads, parts = lax.optimization_barrier((d_heads, parts))
            state = middle + return_blocks(parts) + branch_bias[layer, 1]
        else:
            d_heads, state_low = lax.optimization_barrier((d_heads, state_low))
            mixed = gather_blocks(state_low)
        d_query, d_own, d_far = attend_backward(half, mask, query, own, far, d_heads, logsum)
        if layer == layers - 1:
            d_query, state_low = lax.optimization_barrier((d_query, state.astype(BF)))
        else:
            d_query, mixed = lax.optimization_barrier((d_query, mixed))
            mixed = restored(mixed, ranks_at, BF)
        d_own = d_own + swap(d_far).astype(F32)
        heads_b[layer] = jnp.stack([jnp.sum(d_query, axis=0), jnp.sum(d_own[1], axis=0)])
        d_projected = jnp.concatenate([d_query, d_own[0], d_own[1]], axis=1).astype(BF)
        if layer == layers - 1:
            d_partial = [matmul_t(block, w_in) for block in row_blocks(d_projected)]
            attn_pairs = [(a_low, d_projected), (mid_low, heads_low)]
        else:
            d_partial = matmul_t(d_projected, w_in)
            line = [jnp.sum(d_partial * first_scaled, axis=0), jnp.sum(d_partial, axis=0), shared]
            line += [heads_b[0].reshape(-1), heads_b[1].reshape(-1), units_b[0], units_b[1]]
            line = jnp.concatenate(line)
            line = jnp.pad(line, (0, shard * 256 - line.shape[0])).astype(BF).reshape(shard, 256)
            line = jnp.broadcast_to(line[None], (size, shard, 256)).reshape(size * shard, 256)
            pairs = [(a_low, d_projected), (mid_low, heads_low)]
            mine = merged(*weight_products(pairs, line, half))
            mine, d_partial = lax.optimization_barrier((mine, d_partial))
            d_partial = row_blocks(d_partial)
            moved = jnp.sum(exchange(mine, "dp").astype(F32), axis=0)
            grad_in_first, grad_out_first = moved[:, :w3], moved[:, w3:w4]
            line = moved[:, w4:].reshape(-1)
        d_normed = return_blocks(d_partial)
        d_state, gain_one, shift_one = normalize_back(d_normed, a_scaled, a_inv, norm_gain[layer, 0])
        grad = grad_mid + d_state
        gains[layer] = jnp.stack([gain_one, gain_two])
        shifts[layer] = jnp.stack([shift_one, shift_two])

    later = reduced(matrices[0]).astype(F32)
    all_in = jnp.stack([grad_in_first, later[:, :w3]]).reshape(layers, shard, 3, local_w)
    all_out = jnp.stack([grad_out_first, later[:, w3:w4]])
    all_up = jnp.stack([later[:, w4 : w4 + local_f], early[:, :local_f]])
    all_down = jnp.stack([later[:, w4 + local_f :], early[:, local_f:]])

    token_grad = restored(gather_blocks(grad.astype(BF)), ranks_at, F32)
    cut = 2 * width + 10 * share_w
    lines = by_rank(gather_blocks(line[:cut].reshape(-1, share_w)))
    late = jnp.sum(lines[:, : 2 * ranks], axis=0).reshape(2, width)
    shared = lines[:, 2 * ranks :].transpose(1, 0, 2).reshape(10, width)
    gain_grad = jnp.stack([late[0], shared[4], shared[0], shared[1]]).reshape(layers, 2, width)
    shift_grad = jnp.stack([late[1], shared[5], shared[2], shared[3]]).reshape(layers, 2, width)
    branch_grad = shared[6:10].reshape(layers, 2, width)
    head_grad = line[cut : cut + layers * 2 * local_w].reshape(layers, 2, local_w)
    cut += layers * 2 * local_w
    unit_grad = line[cut : cut + layers * local_f].reshape(layers, local_f)
    return (
        mixed.reshape(1, rows, width),
        token_grad.reshape(1, rows, width),
        all_in,
        all_out,
        all_up,
        all_down,
        gain_grad,
        shift_grad,
        head_grad,
        unit_grad,
        branch_grad,
    )


def solution(mesh):
    return jax.shard_map(
        on_device,
        mesh=mesh,
        in_specs=(
            P("dp", "ctx", None),
            P(None, ("dp", "ctx"), None, "mp"),
            P(None, ("dp", "ctx"), "mp"),
            P(None, ("dp", "ctx"), "mp"),
            P(None, ("dp", "ctx"), "mp"),
            P(),
            P(),
            P(None, None, "mp"),
            P(None, "mp"),
            P(),
            P("dp", "ctx", None),
        ),
        out_specs=(
            P("dp", "ctx", None),
            P("dp", "ctx", None),
            P(None, ("dp", "ctx"), None, "mp"),
            P(None, ("dp", "ctx"), "mp"),
            P(None, ("dp", "ctx"), "mp"),
            P(None, ("dp", "ctx"), "mp"),
            P(),
            P(),
            P(None, None, "mp"),
            P(None, "mp"),
            P(),
        ),
        check_vma=False,
    )
```

```python
from functools import partial

import jax
import jax.numpy as jnp
from jax import lax
from jax.experimental import pallas as pl
from jax.experimental.pallas import tpu as pltpu
from jax.sharding import PartitionSpec as P

HEAD_DIM = 64
EPS = 1e-05
BF = jnp.bfloat16
F32 = jnp.float32
GRID = ("dp", "ctx")
CHUNK = 32
LOG2E = 1.4426950408889634


def matmul(left, right):
    return jnp.dot(left, right, preferred_element_type=F32)


def matmul_t(left, right):
    return lax.dot_general(left, right, (((1,), (1,)), ((), ())), preferred_element_type=F32)


def matmul_tn(left, right):
    return lax.dot_general(left, right, (((0,), (0,)), ((), ())), preferred_element_type=F32)


def normalize_fwd(value, gain, shift):
    mean = jnp.mean(value, axis=-1, keepdims=True)
    centred = value - mean
    variance = jnp.mean(centred * centred, axis=-1, keepdims=True)
    inverse = lax.rsqrt(variance + EPS)
    scaled = centred * inverse
    return (scaled * gain + shift, scaled, inverse)


def normalize_back(grad, scaled, inverse, gain):
    weighted = grad * gain
    first = jnp.mean(weighted, axis=-1, keepdims=True)
    second = jnp.mean(weighted * scaled, axis=-1, keepdims=True)
    return (
        inverse * (weighted - first - scaled * second),
        jnp.sum(grad * scaled, axis=0),
        jnp.sum(grad, axis=0),
    )


def head_lanes(block, head):
    lane = lax.broadcasted_iota(jnp.int32, block.shape, 1)
    return jnp.where((lane >= HEAD_DIM) == (head == 1), block, jnp.zeros_like(block))


def attend_kernel(half_ref, mask_ref, q_ref, own_ref, far_ref, o_ref, lse_ref):
    factor = HEAD_DIM ** (-0.5) * LOG2E

    def run(far):
        out = None
        for head in range(2):
            query = head_lanes(q_ref[...], head)
            near_s = matmul_t(own_ref[0], query) * factor + mask_ref[...]
            top = jnp.max(near_s, axis=0, keepdims=True)
            if far:
                far_s = matmul_t(far_ref[0], query) * factor
                top = jnp.maximum(top, jnp.max(far_s, axis=0, keepdims=True))
            near_p = jnp.exp2(near_s - top)
            total = jnp.sum(near_p, axis=0, keepdims=True)
            mixed = matmul_tn(head_lanes(own_ref[1], head), near_p.astype(BF))
            if far:
                far_p = jnp.exp2(far_s - top)
                total = total + jnp.sum(far_p, axis=0, keepdims=True)
                mixed = mixed + matmul_tn(head_lanes(far_ref[1], head), far_p.astype(BF))
            lse_ref[0, head : head + 1, :] = top + jnp.log2(total)
            mixed = mixed / total
            out = mixed if out is None else out + mixed
        o_ref[...] = out.T.astype(BF)

    pl.when(half_ref[0] == 1)(lambda: run(True))
    pl.when(half_ref[0] == 0)(lambda: run(False))


def attend_back_kernel(
    half_ref, mask_ref, q_ref, own_ref, far_ref, g_ref, lse_ref, dq_ref, down_ref, dfar_ref
):
    scale = HEAD_DIM ** (-0.5)
    factor = scale * LOG2E

    def run(far):
        refs = [own_ref] + ([far_ref] if far else [])
        d_query, d_keys, d_values = None, [None, None], [None, None]
        for head in range(2):
            query, grad = head_lanes(q_ref[...], head), head_lanes(g_ref[...], head)
            lse = lse_ref[0, head : head + 1, :]
            weights, d_weights, inner = [], [], None
            for index, ref in enumerate(refs):
                scores = matmul_t(ref[0], query) * factor - lse
                if index == 0:
                    scores = scores + mask_ref[...]
                weights.append(jnp.exp2(scores))
                d_weights.append(matmul_t(ref[1], grad))
                part = jnp.sum(weights[-1] * d_weights[-1], axis=0, keepdims=True)
                inner = part if inner is None else inner + part
            for index, ref in enumerate(refs):
                d_scores = (weights[index] * (d_weights[index] - inner)).astype(BF)
                part_k = matmul(d_scores, query)
                part_v = matmul(weights[index].astype(BF), grad)
                part_q = matmul_tn(head_lanes(ref[0], head), d_scores)
                d_keys[index] = part_k if d_keys[index] is None else d_keys[index] + part_k
                d_values[index] = part_v if d_values[index] is None else d_values[index] + part_v
                d_query = part_q if d_query is None else d_query + part_q
        dq_ref[...] = d_query.T * scale
        down_ref[0] = d_keys[0] * scale
        down_ref[1] = d_values[0]
        if far:
            dfar_ref[0] = (d_keys[1] * scale).astype(BF)
            dfar_ref[1] = d_values[1].astype(BF)
        else:
            dfar_ref[...] = jnp.zeros(dfar_ref.shape, BF)

    pl.when(half_ref[0] == 1)(lambda: run(True))
    pl.when(half_ref[0] == 0)(lambda: run(False))


def attend_specs(rows):
    pair = 2 * HEAD_DIM
    return (
        pl.BlockSpec(memory_space=pltpu.SMEM),
        pl.BlockSpec((rows, rows), lambda i: (0, 0)),
        pl.BlockSpec((rows, pair), lambda i: (0, i)),
        pl.BlockSpec((2, rows, pair), lambda i: (0, 0, i)),
        pl.BlockSpec((1, 2, rows), lambda i: (i, 0, 0)),
    )


def kernel_params(flops, moved):
    return dict(
        compiler_params=pltpu.CompilerParams(vmem_limit_bytes=40 * 1024 * 1024),
        cost_estimate=pl.CostEstimate(flops=flops, bytes_accessed=moved, transcendentals=0),
    )


def attend_forward(half, mask, query, own, far):
    rows, width = query.shape
    pairs = width // (2 * HEAD_DIM)
    scalar, square, flat, both, line = attend_specs(rows)
    return pl.pallas_call(
        attend_kernel,
        grid=(pairs,),
        in_specs=[scalar, square, flat, both, both],
        out_specs=[flat, line],
        out_shape=[
            jax.ShapeDtypeStruct((rows, width), BF),
            jax.ShapeDtypeStruct((pairs, 2, rows), F32),
        ],
        **kernel_params(1000000000, 4000000),
    )(half, mask, query, own, far)


def attend_backward(half, mask, query, own, far, grad, lse):
    rows, width = query.shape
    pairs = width // (2 * HEAD_DIM)
    scalar, square, flat, both, line = attend_specs(rows)
    return pl.pallas_call(
        attend_back_kernel,
        grid=(pairs,),
        in_specs=[scalar, square, flat, both, both, flat, line],
        out_specs=[flat, both, both],
        out_shape=[
            jax.ShapeDtypeStruct((rows, width), F32),
            jax.ShapeDtypeStruct((2, rows, width), F32),
            jax.ShapeDtypeStruct((2, rows, width), BF),
        ],
        **kernel_params(1000000000, 6000000),
    )(half, mask, query, own, far, grad, lse)


def product_kernel(counts, *refs):
    out_ref, at, column = refs[-1], 0, 0

    def taken(count):
        nonlocal at
        blocks = [ref[...] for ref in refs[at : at + count]]
        at += count
        return blocks[0] if count == 1 else jnp.concatenate(blocks, axis=0)

    for left_count, right_count in counts:
        left, right = taken(left_count), taken(right_count)
        width = right.shape[1]
        out_ref[:, column : column + width] = matmul_tn(left, right).astype(BF)
        column += width
    if at < len(refs) - 1:
        out_ref[:, column:] = refs[at][...]


def split_kernel(counts, half_ref, *refs):
    tile_ref = refs[-1]
    product_kernel(counts, *refs[:-3], tile_ref)
    tall = tile_ref.shape[0]
    step = CHUNK
    mine, other = refs[-3], refs[-2]
    for at in range(0, tall // 2, step):
        first, second = tile_ref[2 * at : 2 * at + step], tile_ref[2 * at + step : 2 * at + 2 * step]
        low = half_ref[0] == 0
        mine[at : at + step] = jnp.where(low, first, second)
        other[at : at + step] = jnp.where(low, second, first)


def weight_products(pairs, extra=None, half=None):
    pairs = [[x if isinstance(x, list) else [x] for x in pair] for pair in pairs]
    height = pairs[0][0][0].shape[1]
    tile = 256
    specs, operands, width = [], [], 0
    for left, right in pairs:
        specs += [pl.BlockSpec((x.shape[0], tile), lambda i: (0, i)) for x in left]
        specs += [pl.BlockSpec(x.shape, lambda i: (0, 0)) for x in right]
        operands += [*left, *right]
        width += right[0].shape[1]
    if extra is not None:
        specs.append(pl.BlockSpec((tile, extra.shape[1]), lambda i: (i, 0)))
        operands.append(extra)
        width += extra.shape[1]
    if half is not None:
        counts = [(len(left), len(right)) for left, right in pairs]
        return pl.pallas_call(
            partial(split_kernel, counts),
            grid=(height // tile,),
            in_specs=[pl.BlockSpec(memory_space=pltpu.SMEM), *specs],
            out_specs=[pl.BlockSpec((tile // 2, width), lambda i: (i, 0))] * 2,
            out_shape=[pltpu.HBM((height // 2, width), BF)] * 2,
            scratch_shapes=[pltpu.VMEM((tile, width), BF)],
            **kernel_params(1000000, 1000000),
        )(half, *operands)
    return pl.pallas_call(
        partial(product_kernel, [(len(left), len(right)) for left, right in pairs]),
        grid=(height // tile,),
        in_specs=specs,
        out_specs=pl.BlockSpec((tile, width), lambda i: (i, 0)),
        out_shape=pltpu.HBM((height, width), BF),
        **kernel_params(1000000, 1000000),
    )(*operands)


def shifted(size, step):
    return [(i, (i + step) % size) for i in range(size)]


def gather_blocks(own):
    size = lax.axis_size("mp")
    return [own] + [lax.ppermute(own, "mp", shifted(size, -step)) for step in range(1, size)]


def gather_rows(own):
    return jnp.concatenate(gather_blocks(own), axis=0)


def return_parts(blocks, beside=None):
    size = lax.axis_size("mp")
    parts = [
        lax.ppermute(blocks[step].astype(BF), "mp", shifted(size, step)) for step in range(1, size)
    ]
    if beside is not None:
        parts, beside = lax.optimization_barrier((parts, beside))
    parts = [blocks[0], *parts]
    return parts if beside is None else (parts, beside)


def return_blocks(blocks):
    parts = return_parts(blocks)
    total = parts[0]
    for part in parts[1:]:
        total = total + part.astype(F32)
    return total


def restore_kernel(rank_ref, *refs):
    for step in range(len(refs) - 1):

        @pl.when(pl.program_id(0) == step)
        def _(step=step):
            refs[-1][...] = refs[step][...].astype(refs[-1].dtype)


def restored(blocks, rank, kind):
    count = len(blocks)
    share, width = blocks[0].shape
    return pl.pallas_call(
        restore_kernel,
        grid_spec=pltpu.PrefetchScalarGridSpec(
            num_scalar_prefetch=1,
            grid=(count,),
            in_specs=[pl.BlockSpec((share, width), lambda i, rank_ref: (0, 0))] * count,
            out_specs=pl.BlockSpec(
                (share, width), lambda i, rank_ref: (lax.rem(i + rank_ref[0], count), 0)
            ),
        ),
        out_shape=jax.ShapeDtypeStruct((count * share, width), kind),
        **kernel_params(1000000, 1000000),
    )(rank, *blocks)


def finish_kernel(last_ref, early_ref, later_ref, in_ref, out_ref, up_ref, down_ref):
    w1 = in_ref.shape[3]
    for part in range(3):
        at = slice(part * w1, (part + 1) * w1)
        in_ref[0, part] = last_ref[:, at]
        in_ref[1, part] = later_ref[:, at].astype(F32)
    w3, w4, wide = 3 * w1, 4 * w1, up_ref.shape[2]
    out_ref[0] = last_ref[:, w3:w4]
    out_ref[1] = later_ref[:, w3:w4].astype(F32)
    up_ref[0] = later_ref[:, w4 : w4 + wide].astype(F32)
    down_ref[0] = later_ref[:, w4 + wide :].astype(F32)
    up_ref[1] = early_ref[:, :wide].astype(F32)
    down_ref[1] = early_ref[:, wide:].astype(F32)


def finished(last, early, later, width, wide):
    rows = last.shape[0]
    shapes = [(2, 3, rows, width), (2, rows, width), (2, rows, wide), (2, rows, wide)]
    outs = pl.pallas_call(
        finish_kernel,
        out_shape=[jax.ShapeDtypeStruct(shape, F32) for shape in shapes],
        **kernel_params(1000000, 1000000),
    )(last, early, later)
    return [outs[0].transpose(0, 2, 1, 3), *outs[1:]]


def norm_back_kernel(own_ref, one_ref, two_ref, three_ref, value_ref, grad_ref, gain_ref, mid_ref, low_ref, sums_ref):
    incoming = own_ref[...]
    for ref in (one_ref, two_ref, three_ref):
        incoming = incoming + ref[...].astype(F32)
    value = value_ref[...]
    centred = value - jnp.mean(value, axis=-1, keepdims=True)
    inverse = lax.rsqrt(jnp.mean(centred * centred, axis=-1, keepdims=True) + EPS)
    scaled = centred * inverse
    weighted = incoming * gain_ref[...]
    first = jnp.mean(weighted, axis=-1, keepdims=True)
    second = jnp.mean(weighted * scaled, axis=-1, keepdims=True)
    mid = grad_ref[...] + inverse * (weighted - first - scaled * second)
    mid_ref[...] = mid
    low_ref[...] = mid.astype(BF)
    sums_ref[0:1] = jnp.sum(incoming * scaled, axis=0, keepdims=True)
    sums_ref[1:2] = jnp.sum(incoming, axis=0, keepdims=True)
    sums_ref[2:3] = jnp.sum(mid, axis=0, keepdims=True)


def norm_back(parts, value, grad, gain):
    shape = value.shape
    return pl.pallas_call(
        norm_back_kernel,
        out_shape=[
            jax.ShapeDtypeStruct(shape, F32),
            jax.ShapeDtypeStruct(shape, BF),
            jax.ShapeDtypeStruct((3, shape[1]), F32),
        ],
        **kernel_params(1000000, 1000000),
    )(*parts, value, grad, gain[None])


def merged(mine, other):
    return (mine.astype(F32) + swap(other).astype(F32)).astype(BF)


def by_rank(blocks):
    size = lax.axis_size("mp")
    start = lax.rem(size - lax.axis_index("mp"), size)
    return lax.dynamic_slice_in_dim(jnp.stack(blocks + blocks), start, size, 0)


def row_blocks(value):
    share = value.shape[0] // lax.axis_size("mp")
    return [value[at : at + share] for at in range(0, value.shape[0], share)]


def swap(value):
    return lax.ppermute(value, "ctx", [(0, 1), (1, 0)])


def spread(shard, half):
    size = lax.axis_size("dp")
    rows, width = shard.shape
    other = swap(shard)
    first = half == 0
    both = jnp.concatenate([jnp.where(first, shard, other), jnp.where(first, other, shard)], axis=0)
    both = jnp.where(first, both[:, : width // 2], both[:, width // 2 :])
    copies = jnp.broadcast_to(both[None], (size, 2 * rows, width // 2))
    mine = lax.all_to_all(copies, "dp", 0, 0, tiled=True).reshape(size * 2 * rows, width // 2)
    other = swap(mine)
    return jnp.concatenate([jnp.where(first, mine, other), jnp.where(first, other, mine)], axis=1)


def exchange(value, axes):
    size = lax.axis_size(axes)
    parts = value.reshape(size, value.shape[0] // size, value.shape[1])
    return lax.all_to_all(parts, axes, 0, 0, tiled=True)


def on_device(
    tokens,
    attn_in,
    attn_out,
    mlp_in,
    mlp_out,
    norm_gain,
    norm_shift,
    head_bias,
    unit_bias,
    branch_bias,
    cotangent,
):
    _, rows, width = tokens.shape
    layers, shard, _, local_w = attn_in.shape
    local_f = mlp_in.shape[2]
    ranks = lax.axis_size("mp")
    rank = lax.axis_index("mp")
    half = lax.axis_index("ctx")
    share = rows // ranks
    share_w = width // ranks

    def rotated(block):
        return lax.dynamic_slice_in_dim(jnp.concatenate([block, block], axis=0), rank * share, rows, 0)

    place = (jnp.arange(rows) + rank * share) % rows
    mask = jnp.where(place[:, None] <= place[None, :], 0.0, -1e30).astype(F32)
    ranks_at = rank.reshape(1)

    flat_in = attn_in.reshape(layers, shard, 3 * local_w)
    first = spread(jnp.concatenate([flat_in[0], attn_out[0]], axis=1), half)
    packed = jnp.concatenate([mlp_in[0], mlp_out[0]], axis=1)
    near = lax.all_gather(packed, GRID, axis=0, tiled=True)
    packed = jnp.concatenate([flat_in[1], attn_out[1], mlp_in[1], mlp_out[1]], axis=1)
    rest = lax.all_gather(packed, GRID, axis=0, tiled=True)
    w3, w4 = 3 * local_w, 4 * local_w
    weights = [
        (first[:, :w3], first[:, w3:], near[:, :local_f], near[:, local_f:]),
        (rest[:, :w3], rest[:, w3:w4], rest[:, w4 : w4 + local_f], rest[:, w4 + local_f :]),
    ]

    half = half.reshape(1)
    low_tokens = rotated(tokens.reshape(rows, width))
    state = low_tokens[:share].astype(F32)
    saved = []
    for layer in range(layers):
        w_in, w_out, w_up, w_down = weights[layer]
        if layer == 0:
            normed, scaled_all, inv_all = normalize_fwd(
                low_tokens.astype(F32), norm_gain[layer, 0], norm_shift[layer, 0]
            )
            a_low, a_scaled, a_inv = normed.astype(BF), scaled_all[:share], inv_all[:share]
            first_scaled = scaled_all
        else:
            normed, a_scaled, a_inv = normalize_fwd(state, norm_gain[layer, 0], norm_shift[layer, 0])
            a_low = gather_rows(normed.astype(BF))
        projected = matmul(a_low, w_in)
        query = (projected[:, :local_w] + head_bias[layer, 0]).astype(BF)
        keys = projected[:, local_w : 2 * local_w].astype(BF)
        values = (projected[:, 2 * local_w :] + head_bias[layer, 1]).astype(BF)
        own = jnp.stack([keys, values])
        far = swap(own)
        heads_low, logsum = attend_forward(half, mask, query, own, far)
        if layer == 0:
            parts = row_blocks(matmul_t(heads_low, w_out))
        else:
            parts = [matmul_t(block, w_out) for block in row_blocks(heads_low)]
        middle = state + return_blocks(parts) + branch_bias[layer, 0]
        second, _, _ = normalize_fwd(middle, norm_gain[layer, 1], norm_shift[layer, 1])
        c_low = gather_blocks(second.astype(BF))
        hidden = [matmul(block, w_up) + unit_bias[layer] for block in c_low]
        active = [jax.nn.gelu(block, approximate=True).astype(BF) for block in hidden]
        if layer < layers - 1:
            parts = [matmul_t(block, w_down) for block in active]
            state = middle + return_blocks(parts) + branch_bias[layer, 1]
        saved.append(
            (a_low, a_scaled, a_inv, query, own, far, logsum, heads_low)
            + (c_low, middle, hidden, active)
        )
    grad_low = rotated(cotangent.reshape(rows, width))
    grad_low = row_blocks(grad_low)
    grad = grad_low[0].astype(F32)
    gains, shifts, heads_b, units_b, branches_b, matrices = {}, {}, {}, {}, {}, {}
    def reduced(packed):
        return lax.psum_scatter(packed, GRID, scatter_dimension=0, tiled=True)

    size = lax.axis_size(GRID)
    attn_pairs = []
    for layer in reversed(range(layers)):
        w_in, w_out, w_up, w_down = weights[layer]
        a_low, a_scaled, a_inv, query, own, far, logsum, heads_low = saved[layer][:8]
        c_low, c_value, hidden, active = saved[layer][8:]
        if layer < layers - 1:
            grad_low = gather_blocks(grad.astype(BF))
        bias_down = jnp.sum(grad, axis=0)
        d_hidden = []
        for block, low in zip(hidden, grad_low, strict=True):
            gelu_pull = jax.vjp(partial(jax.nn.gelu, approximate=True), block)[1]
            d_hidden.append(gelu_pull(matmul(low, w_down))[0])
        units_b[layer] = sum(jnp.sum(block, axis=0) for block in d_hidden)
        hidden_low = [block.astype(BF) for block in d_hidden]
        parts = [matmul_t(block, w_up) for block in hidden_low]
        products = weight_products(attn_pairs + [(c_low, hidden_low), (grad_low, active)])
        if layer == layers - 1:
            d_second, products = return_parts(parts, products)
        else:
            d_second, (products, early) = return_parts(parts, (products, reduced(matrices[1])))
        matrices[layer] = products
        grad_mid, mid_own, sums = norm_back(d_second, c_value, grad, norm_gain[layer, 1])
        gain_two, shift_two, bias_attn = sums[0], sums[1], sums[2]
        branches_b[layer] = jnp.stack([bias_attn, bias_down])
        if layer == layers - 1:
            mid_own, active[0] = lax.optimization_barrier((mid_own, active[0]))
            parts = row_blocks(matmul_t(jnp.concatenate(active, axis=0), w_down))
            parts = parts[:1] + [part.astype(BF) for part in parts[1:]]
            mid_low = gather_rows(mid_own)
        else:
            shared = [gains[1], shifts[1], gain_two[None], shift_two[None], branches_b[0], branches_b[1]]
            shared = jnp.pad(jnp.concatenate(shared), ((0, 6), (0, 0))).astype(BF)
            blocks = gather_blocks(jnp.concatenate([mid_own, shared], axis=0))
            mid_low = jnp.concatenate([block[:share] for block in blocks], axis=0)
            shared = sum(block[share : share + 10].astype(F32) for block in blocks)
            shared = shared.reshape(10, ranks, share_w)
            shared = lax.dynamic_index_in_dim(shared, rank, 1, False).reshape(-1)
        d_heads = matmul(mid_low, w_out).astype(BF)
        if layer == layers - 1:
            d_heads, parts = lax.optimization_barrier((d_heads, parts))
            state = middle + return_blocks(parts) + branch_bias[layer, 1]
        else:
            d_heads, state_low = lax.optimization_barrier((d_heads, state_low))
            mixed = gather_blocks(state_low)
        d_query, d_own, d_far = attend_backward(half, mask, query, own, far, d_heads, logsum)
        if layer == layers - 1:
            d_query, state_low = lax.optimization_barrier((d_query, state.astype(BF)))
        else:
            d_query, mixed = lax.optimization_barrier((d_query, mixed))
            mixed = restored(mixed, ranks_at, BF)
        d_own = d_own + swap(d_far).astype(F32)
        heads_b[layer] = jnp.stack([jnp.sum(d_query, axis=0), jnp.sum(d_own[1], axis=0)])
        d_projected = jnp.concatenate([d_query, d_own[0], d_own[1]], axis=1).astype(BF)
        if layer == layers - 1:
            d_partial = [matmul_t(block, w_in) for block in row_blocks(d_projected)]
            attn_pairs = [(a_low, d_projected), (mid_low, heads_low)]
        else:
            d_partial = matmul_t(d_projected, w_in)
            line = [jnp.sum(d_partial * first_scaled, axis=0), jnp.sum(d_partial, axis=0), shared]
            line += [heads_b[0].reshape(-1), heads_b[1].reshape(-1), units_b[0], units_b[1]]
            line = jnp.concatenate(line)
            line = jnp.pad(line, (0, shard * 256 - line.shape[0])).astype(BF).reshape(shard, 256)
            line = jnp.broadcast_to(line[None], (size, shard, 256)).reshape(size * shard, 256)
            pairs = [(a_low, d_projected), (mid_low, heads_low)]
            (mine, other), d_partial = lax.optimization_barrier(
                (weight_products(pairs, line, half), d_partial)
            )
            mine = merged(mine, other)
            d_partial = row_blocks(d_partial)
            moved = jnp.sum(exchange(mine, "dp").astype(F32), axis=0)
            last = moved[:, :w4]
            line = moved[:, w4:].reshape(-1)
        d_normed = return_blocks(d_partial)
        d_state, gain_one, shift_one = normalize_back(d_normed, a_scaled, a_inv, norm_gain[layer, 0])
        grad = grad_mid + d_state
        gains[layer] = jnp.stack([gain_one, gain_two])
        shifts[layer] = jnp.stack([shift_one, shift_two])

    later = reduced(matrices[0])
    all_in, all_out, all_up, all_down = finished(last, early, later, local_w, local_f)

    token_grad = restored(gather_blocks(grad.astype(BF)), ranks_at, F32)
    cut = 2 * width + 10 * share_w
    lines = by_rank(gather_blocks(line[:cut].reshape(-1, share_w)))
    late = jnp.sum(lines[:, : 2 * ranks], axis=0).reshape(2, width)
    shared = lines[:, 2 * ranks :].transpose(1, 0, 2).reshape(10, width)
    gain_grad = jnp.stack([late[0], shared[4], shared[0], shared[1]]).reshape(layers, 2, width)
    shift_grad = jnp.stack([late[1], shared[5], shared[2], shared[3]]).reshape(layers, 2, width)
    branch_grad = shared[6:10].reshape(layers, 2, width)
    head_grad = line[cut : cut + layers * 2 * local_w].reshape(layers, 2, local_w)
    cut += layers * 2 * local_w
    unit_grad = line[cut : cut + layers * local_f].reshape(layers, local_f)
    return (
        mixed.reshape(1, rows, width),
        token_grad.reshape(1, rows, width),
        all_in,
        all_out,
        all_up,
        all_down,
        gain_grad,
        shift_grad,
        head_grad,
        unit_grad,
        branch_grad,
    )


def solution(mesh):
    return jax.shard_map(
        on_device,
        mesh=mesh,
        in_specs=(
            P("dp", "ctx", None),
            P(None, ("dp", "ctx"), None, "mp"),
            P(None, ("dp", "ctx"), "mp"),
            P(None, ("dp", "ctx"), "mp"),
            P(None, ("dp", "ctx"), "mp"),
            P(),
            P(),
            P(None, None, "mp"),
            P(None, "mp"),
            P(),
            P("dp", "ctx", None),
        ),
        out_specs=(
            P("dp", "ctx", None),
            P("dp", "ctx", None),
            P(None, ("dp", "ctx"), None, "mp"),
            P(None, ("dp", "ctx"), "mp"),
            P(None, ("dp", "ctx"), "mp"),
            P(None, ("dp", "ctx"), "mp"),
            P(),
            P(),
            P(None, None, "mp"),
            P(None, "mp"),
            P(),
        ),
        check_vma=False,
    )
```

```python
from functools import partial

import jax
import jax.numpy as jnp
from jax import lax
from jax.experimental import pallas as pl
from jax.experimental.pallas import tpu as pltpu
from jax.sharding import PartitionSpec as P

HEAD_DIM = 64
EPS = 1e-05
BF = jnp.bfloat16
F32 = jnp.float32
GRID = ("dp", "ctx")
CHUNK = 32
LOG2E = 1.4426950408889634


def matmul(left, right):
    return jnp.dot(left, right, preferred_element_type=F32)


def matmul_t(left, right):
    return lax.dot_general(left, right, (((1,), (1,)), ((), ())), preferred_element_type=F32)


def matmul_tn(left, right):
    return lax.dot_general(left, right, (((0,), (0,)), ((), ())), preferred_element_type=F32)


def normalize_fwd(value, gain, shift):
    mean = jnp.mean(value, axis=-1, keepdims=True)
    centred = value - mean
    variance = jnp.mean(centred * centred, axis=-1, keepdims=True)
    inverse = lax.rsqrt(variance + EPS)
    scaled = centred * inverse
    return (scaled * gain + shift, scaled, inverse)


def normalize_back(grad, scaled, inverse, gain):
    weighted = grad * gain
    first = jnp.mean(weighted, axis=-1, keepdims=True)
    second = jnp.mean(weighted * scaled, axis=-1, keepdims=True)
    return (
        inverse * (weighted - first - scaled * second),
        jnp.sum(grad * scaled, axis=0),
        jnp.sum(grad, axis=0),
    )


def head_lanes(block, head):
    lane = lax.broadcasted_iota(jnp.int32, block.shape, 1)
    return jnp.where((lane >= HEAD_DIM) == (head == 1), block, jnp.zeros_like(block))


def attend_kernel(half_ref, mask_ref, q_ref, own_ref, far_ref, o_ref, lse_ref):
    factor = HEAD_DIM ** (-0.5) * LOG2E

    def run(far):
        out = None
        for head in range(2):
            query = head_lanes(q_ref[...], head)
            near_s = matmul_t(own_ref[0], query) * factor + mask_ref[...]
            top = jnp.max(near_s, axis=0, keepdims=True)
            if far:
                far_s = matmul_t(far_ref[0], query) * factor
                top = jnp.maximum(top, jnp.max(far_s, axis=0, keepdims=True))
            near_p = jnp.exp2(near_s - top)
            total = jnp.sum(near_p, axis=0, keepdims=True)
            mixed = matmul_tn(head_lanes(own_ref[1], head), near_p.astype(BF))
            if far:
                far_p = jnp.exp2(far_s - top)
                total = total + jnp.sum(far_p, axis=0, keepdims=True)
                mixed = mixed + matmul_tn(head_lanes(far_ref[1], head), far_p.astype(BF))
            lse_ref[0, head : head + 1, :] = top + jnp.log2(total)
            mixed = mixed / total
            out = mixed if out is None else out + mixed
        o_ref[...] = out.T.astype(BF)

    pl.when(half_ref[0] == 1)(lambda: run(True))
    pl.when(half_ref[0] == 0)(lambda: run(False))


def attend_back_kernel(
    half_ref, mask_ref, q_ref, own_ref, far_ref, g_ref, lse_ref, dq_ref, down_ref, dfar_ref
):
    scale = HEAD_DIM ** (-0.5)
    factor = scale * LOG2E

    def run(far):
        refs = [own_ref] + ([far_ref] if far else [])
        d_query, d_keys, d_values = None, [None, None], [None, None]
        for head in range(2):
            query, grad = head_lanes(q_ref[...], head), head_lanes(g_ref[...], head)
            lse = lse_ref[0, head : head + 1, :]
            weights, d_weights, inner = [], [], None
            for index, ref in enumerate(refs):
                scores = matmul_t(ref[0], query) * factor - lse
                if index == 0:
                    scores = scores + mask_ref[...]
                weights.append(jnp.exp2(scores))
                d_weights.append(matmul_t(ref[1], grad))
                part = jnp.sum(weights[-1] * d_weights[-1], axis=0, keepdims=True)
                inner = part if inner is None else inner + part
            for index, ref in enumerate(refs):
                d_scores = (weights[index] * (d_weights[index] - inner)).astype(BF)
                part_k = matmul(d_scores, query)
                part_v = matmul(weights[index].astype(BF), grad)
                part_q = matmul_tn(head_lanes(ref[0], head), d_scores)
                d_keys[index] = part_k if d_keys[index] is None else d_keys[index] + part_k
                d_values[index] = part_v if d_values[index] is None else d_values[index] + part_v
                d_query = part_q if d_query is None else d_query + part_q
        dq_ref[...] = d_query.T * scale
        down_ref[0] = d_keys[0] * scale
        down_ref[1] = d_values[0]
        if far:
            dfar_ref[0] = (d_keys[1] * scale).astype(BF)
            dfar_ref[1] = d_values[1].astype(BF)
        else:
            dfar_ref[...] = jnp.zeros(dfar_ref.shape, BF)

    pl.when(half_ref[0] == 1)(lambda: run(True))
    pl.when(half_ref[0] == 0)(lambda: run(False))


def attend_specs(rows):
    pair = 2 * HEAD_DIM
    return (
        pl.BlockSpec(memory_space=pltpu.SMEM),
        pl.BlockSpec((rows, rows), lambda i: (0, 0)),
        pl.BlockSpec((rows, pair), lambda i: (0, i)),
        pl.BlockSpec((2, rows, pair), lambda i: (0, 0, i)),
        pl.BlockSpec((1, 2, rows), lambda i: (i, 0, 0)),
    )


def kernel_params(flops, moved):
    return dict(
        compiler_params=pltpu.CompilerParams(vmem_limit_bytes=40 * 1024 * 1024),
        cost_estimate=pl.CostEstimate(flops=flops, bytes_accessed=moved, transcendentals=0),
    )


def attend_forward(half, mask, query, own, far):
    rows, width = query.shape
    pairs = width // (2 * HEAD_DIM)
    scalar, square, flat, both, line = attend_specs(rows)
    return pl.pallas_call(
        attend_kernel,
        grid=(pairs,),
        in_specs=[scalar, square, flat, both, both],
        out_specs=[flat, line],
        out_shape=[
            jax.ShapeDtypeStruct((rows, width), BF),
            jax.ShapeDtypeStruct((pairs, 2, rows), F32),
        ],
        **kernel_params(1000000000, 4000000),
    )(half, mask, query, own, far)


def attend_backward(half, mask, query, own, far, grad, lse):
    rows, width = query.shape
    pairs = width // (2 * HEAD_DIM)
    scalar, square, flat, both, line = attend_specs(rows)
    return pl.pallas_call(
        attend_back_kernel,
        grid=(pairs,),
        in_specs=[scalar, square, flat, both, both, flat, line],
        out_specs=[flat, both, both],
        out_shape=[
            jax.ShapeDtypeStruct((rows, width), F32),
            jax.ShapeDtypeStruct((2, rows, width), F32),
            jax.ShapeDtypeStruct((2, rows, width), BF),
        ],
        **kernel_params(1000000000, 6000000),
    )(half, mask, query, own, far, grad, lse)


def product_kernel(counts, *refs):
    out_ref, at, column = refs[-1], 0, 0

    def taken(count):
        nonlocal at
        blocks = [ref[...] for ref in refs[at : at + count]]
        at += count
        return blocks[0] if count == 1 else jnp.concatenate(blocks, axis=0)

    for left_count, right_count in counts:
        left, right = taken(left_count), taken(right_count)
        width = right.shape[1]
        out_ref[:, column : column + width] = matmul_tn(left, right).astype(BF)
        column += width
    if at < len(refs) - 1:
        out_ref[:, column:] = refs[at][...]


def split_kernel(counts, half_ref, *refs):
    tile_ref = refs[-1]
    product_kernel(counts, *refs[:-3], tile_ref)
    tall = tile_ref.shape[0]
    step = CHUNK
    mine, other = refs[-3], refs[-2]
    for at in range(0, tall // 2, step):
        first, second = tile_ref[2 * at : 2 * at + step], tile_ref[2 * at + step : 2 * at + 2 * step]
        low = half_ref[0] == 0
        mine[at : at + step] = jnp.where(low, first, second)
        other[at : at + step] = jnp.where(low, second, first)


def weight_products(pairs, extra=None, half=None):
    pairs = [[x if isinstance(x, list) else [x] for x in pair] for pair in pairs]
    height = pairs[0][0][0].shape[1]
    tile = 256
    specs, operands, width = [], [], 0
    for left, right in pairs:
        specs += [pl.BlockSpec((x.shape[0], tile), lambda i: (0, i)) for x in left]
        specs += [pl.BlockSpec(x.shape, lambda i: (0, 0)) for x in right]
        operands += [*left, *right]
        width += right[0].shape[1]
    if extra is not None:
        specs.append(pl.BlockSpec((tile, extra.shape[1]), lambda i: (i, 0)))
        operands.append(extra)
        width += extra.shape[1]
    if half is not None:
        counts = [(len(left), len(right)) for left, right in pairs]
        return pl.pallas_call(
            partial(split_kernel, counts),
            grid=(height // tile,),
            in_specs=[pl.BlockSpec(memory_space=pltpu.SMEM), *specs],
            out_specs=[pl.BlockSpec((tile // 2, width), lambda i: (i, 0))] * 2,
            out_shape=[pltpu.HBM((height // 2, width), BF)] * 2,
            scratch_shapes=[pltpu.VMEM((tile, width), BF)],
            **kernel_params(1000000, 1000000),
        )(half, *operands)
    return pl.pallas_call(
        partial(product_kernel, [(len(left), len(right)) for left, right in pairs]),
        grid=(height // tile,),
        in_specs=specs,
        out_specs=pl.BlockSpec((tile, width), lambda i: (i, 0)),
        out_shape=pltpu.HBM((height, width), BF),
        **kernel_params(1000000, 1000000),
    )(*operands)


def shifted(size, step):
    return [(i, (i + step) % size) for i in range(size)]


def gather_blocks(own):
    size = lax.axis_size("mp")
    return [own] + [lax.ppermute(own, "mp", shifted(size, -step)) for step in range(1, size)]


def gather_rows(own):
    return jnp.concatenate(gather_blocks(own), axis=0)


def return_parts(blocks, beside=None):
    size = lax.axis_size("mp")
    parts = [
        lax.ppermute(blocks[step].astype(BF), "mp", shifted(size, step)) for step in range(1, size)
    ]
    parts = [blocks[0], *parts]
    if beside is not None:
        parts, beside = lax.optimization_barrier((parts, beside))
    return parts if beside is None else (parts, beside)


def return_blocks(blocks):
    parts = return_parts(blocks)
    total = parts[0]
    for part in parts[1:]:
        total = total + part.astype(F32)
    return total


def restore_kernel(rank_ref, *refs):
    for step in range(len(refs) - 1):

        @pl.when(pl.program_id(0) == step)
        def _(step=step):
            refs[-1][...] = refs[step][...].astype(refs[-1].dtype)


def restored(blocks, rank, kind):
    count = len(blocks)
    share, width = blocks[0].shape
    return pl.pallas_call(
        restore_kernel,
        grid_spec=pltpu.PrefetchScalarGridSpec(
            num_scalar_prefetch=1,
            grid=(count,),
            in_specs=[pl.BlockSpec((share, width), lambda i, rank_ref: (0, 0))] * count,
            out_specs=pl.BlockSpec(
                (share, width), lambda i, rank_ref: (lax.rem(i + rank_ref[0], count), 0)
            ),
        ),
        out_shape=jax.ShapeDtypeStruct((count * share, width), kind),
        **kernel_params(1000000, 1000000),
    )(rank, *blocks)


def finish_kernel(last_ref, early_ref, later_ref, in_ref, out_ref, up_ref, down_ref):
    w1 = in_ref.shape[3]
    for part in range(3):
        at = slice(part * w1, (part + 1) * w1)
        in_ref[0, part] = last_ref[:, at]
        in_ref[1, part] = later_ref[:, at].astype(F32)
    w3, w4, wide = 3 * w1, 4 * w1, up_ref.shape[2]
    out_ref[0] = last_ref[:, w3:w4]
    out_ref[1] = later_ref[:, w3:w4].astype(F32)
    up_ref[0] = later_ref[:, w4 : w4 + wide].astype(F32)
    down_ref[0] = later_ref[:, w4 + wide :].astype(F32)
    up_ref[1] = early_ref[:, :wide].astype(F32)
    down_ref[1] = early_ref[:, wide:].astype(F32)


def finished(last, early, later, width, wide):
    rows = last.shape[0]
    shapes = [(2, 3, rows, width), (2, rows, width), (2, rows, wide), (2, rows, wide)]
    outs = pl.pallas_call(
        finish_kernel,
        out_shape=[jax.ShapeDtypeStruct(shape, F32) for shape in shapes],
        **kernel_params(1000000, 1000000),
    )(last, early, later)
    return [outs[0].transpose(0, 2, 1, 3), *outs[1:]]


def norm_back_kernel(own_ref, one_ref, two_ref, three_ref, value_ref, grad_ref, gain_ref, mid_ref, low_ref, sums_ref):
    incoming = own_ref[...]
    for ref in (one_ref, two_ref, three_ref):
        incoming = incoming + ref[...].astype(F32)
    value = value_ref[...]
    centred = value - jnp.mean(value, axis=-1, keepdims=True)
    inverse = lax.rsqrt(jnp.mean(centred * centred, axis=-1, keepdims=True) + EPS)
    scaled = centred * inverse
    weighted = incoming * gain_ref[...]
    first = jnp.mean(weighted, axis=-1, keepdims=True)
    second = jnp.mean(weighted * scaled, axis=-1, keepdims=True)
    mid = grad_ref[...] + inverse * (weighted - first - scaled * second)
    mid_ref[...] = mid
    low_ref[...] = mid.astype(BF)
    sums_ref[0:1] = jnp.sum(incoming * scaled, axis=0, keepdims=True)
    sums_ref[1:2] = jnp.sum(incoming, axis=0, keepdims=True)
    sums_ref[2:3] = jnp.sum(mid, axis=0, keepdims=True)


def norm_back(parts, value, grad, gain):
    shape = value.shape
    return pl.pallas_call(
        norm_back_kernel,
        out_shape=[
            jax.ShapeDtypeStruct(shape, F32),
            jax.ShapeDtypeStruct(shape, BF),
            jax.ShapeDtypeStruct((3, shape[1]), F32),
        ],
        **kernel_params(1000000, 1000000),
    )(*parts, value, grad, gain[None])


def merged(mine, other):
    return (mine.astype(F32) + swap(other).astype(F32)).astype(BF)


def by_rank(blocks):
    size = lax.axis_size("mp")
    start = lax.rem(size - lax.axis_index("mp"), size)
    return lax.dynamic_slice_in_dim(jnp.stack(blocks + blocks), start, size, 0)


def row_blocks(value):
    share = value.shape[0] // lax.axis_size("mp")
    return [value[at : at + share] for at in range(0, value.shape[0], share)]


def swap(value):
    return lax.ppermute(value, "ctx", [(0, 1), (1, 0)])


def spread(shard, half):
    size = lax.axis_size("dp")
    rows, width = shard.shape
    other = swap(shard)
    first = half == 0
    both = jnp.concatenate([jnp.where(first, shard, other), jnp.where(first, other, shard)], axis=0)
    both = jnp.where(first, both[:, : width // 2], both[:, width // 2 :])
    copies = jnp.broadcast_to(both[None], (size, 2 * rows, width // 2))
    mine = lax.all_to_all(copies, "dp", 0, 0, tiled=True).reshape(size * 2 * rows, width // 2)
    other = swap(mine)
    return jnp.concatenate([jnp.where(first, mine, other), jnp.where(first, other, mine)], axis=1)


def exchange(value, axes):
    size = lax.axis_size(axes)
    parts = value.reshape(size, value.shape[0] // size, value.shape[1])
    return lax.all_to_all(parts, axes, 0, 0, tiled=True)


def on_device(
    tokens,
    attn_in,
    attn_out,
    mlp_in,
    mlp_out,
    norm_gain,
    norm_shift,
    head_bias,
    unit_bias,
    branch_bias,
    cotangent,
):
    _, rows, width = tokens.shape
    layers, shard, _, local_w = attn_in.shape
    local_f = mlp_in.shape[2]
    ranks = lax.axis_size("mp")
    rank = lax.axis_index("mp")
    half = lax.axis_index("ctx")
    share = rows // ranks
    share_w = width // ranks

    def rotated(block):
        return lax.dynamic_slice_in_dim(jnp.concatenate([block, block], axis=0), rank * share, rows, 0)

    place = (jnp.arange(rows) + rank * share) % rows
    mask = jnp.where(place[:, None] <= place[None, :], 0.0, -1e30).astype(F32)
    ranks_at = rank.reshape(1)

    flat_in = attn_in.reshape(layers, shard, 3 * local_w)
    first = spread(jnp.concatenate([flat_in[0], attn_out[0]], axis=1), half)
    packed = jnp.concatenate([mlp_in[0], mlp_out[0]], axis=1)
    near = lax.all_gather(packed, GRID, axis=0, tiled=True)
    packed = jnp.concatenate([flat_in[1], attn_out[1], mlp_in[1], mlp_out[1]], axis=1)
    rest = lax.all_gather(packed, GRID, axis=0, tiled=True)
    w3, w4 = 3 * local_w, 4 * local_w
    weights = [
        (first[:, :w3], first[:, w3:], near[:, :local_f], near[:, local_f:]),
        (rest[:, :w3], rest[:, w3:w4], rest[:, w4 : w4 + local_f], rest[:, w4 + local_f :]),
    ]

    half = half.reshape(1)
    low_tokens = rotated(tokens.reshape(rows, width))
    state = low_tokens[:share].astype(F32)
    saved = []
    for layer in range(layers):
        w_in, w_out, w_up, w_down = weights[layer]
        before = state
        if layer == 0:
            normed, first_scaled, first_inv = normalize_fwd(
                low_tokens.astype(F32), norm_gain[layer, 0], norm_shift[layer, 0]
            )
            a_low = normed.astype(BF)
        else:
            normed, _, _ = normalize_fwd(state, norm_gain[layer, 0], norm_shift[layer, 0])
            a_low = gather_rows(normed.astype(BF))
        projected = matmul(a_low, w_in)
        query = (projected[:, :local_w] + head_bias[layer, 0]).astype(BF)
        keys = projected[:, local_w : 2 * local_w].astype(BF)
        values = (projected[:, 2 * local_w :] + head_bias[layer, 1]).astype(BF)
        own = jnp.stack([keys, values])
        far = swap(own)
        heads_low, logsum = attend_forward(half, mask, query, own, far)
        if layer == 0:
            parts = row_blocks(matmul_t(heads_low, w_out))
        else:
            parts = [matmul_t(block, w_out) for block in row_blocks(heads_low)]
        middle = state + return_blocks(parts) + branch_bias[layer, 0]
        second, _, _ = normalize_fwd(middle, norm_gain[layer, 1], norm_shift[layer, 1])
        c_low = gather_blocks(second.astype(BF))
        hidden = [matmul(block, w_up) + unit_bias[layer] for block in c_low]
        active = [jax.nn.gelu(block, approximate=True).astype(BF) for block in hidden]
        if layer < layers - 1:
            parts = [matmul_t(block, w_down) for block in active]
            state = middle + return_blocks(parts) + branch_bias[layer, 1]
        saved.append(
            (a_low, before, query, own, far, logsum, heads_low)
            + (c_low, middle, hidden, active)
        )
    grad_low = rotated(cotangent.reshape(rows, width))
    grad_low = row_blocks(grad_low)
    grad = grad_low[0].astype(F32)
    gains, shifts, heads_b, units_b, branches_b, matrices = {}, {}, {}, {}, {}, {}
    def reduced(packed):
        return lax.psum_scatter(packed, GRID, scatter_dimension=0, tiled=True)

    size = lax.axis_size(GRID)
    attn_pairs = []
    for layer in reversed(range(layers)):
        w_in, w_out, w_up, w_down = weights[layer]
        a_low, a_value, query, own, far, logsum, heads_low = saved[layer][:7]
        c_low, c_value, hidden, active = saved[layer][7:]
        if layer < layers - 1:
            grad_low = gather_blocks(own_low)
        bias_down = jnp.sum(grad, axis=0)
        d_hidden = []
        for block, low in zip(hidden, grad_low, strict=True):
            gelu_pull = jax.vjp(partial(jax.nn.gelu, approximate=True), block)[1]
            d_hidden.append(gelu_pull(matmul(low, w_down))[0])
        units_b[layer] = sum(jnp.sum(block, axis=0) for block in d_hidden)
        hidden_low = [block.astype(BF) for block in d_hidden]
        parts = [matmul_t(block, w_up) for block in hidden_low]
        products = weight_products(attn_pairs + [(c_low, hidden_low), (grad_low, active)])
        if layer == layers - 1:
            d_second, products = return_parts(parts, products)
        else:
            d_second, (products, early) = return_parts(parts, (products, reduced(matrices[1])))
        matrices[layer] = products
        grad_mid, mid_own, sums = norm_back(d_second, c_value, grad, norm_gain[layer, 1])
        gain_two, shift_two, bias_attn = sums[0], sums[1], sums[2]
        branches_b[layer] = jnp.stack([bias_attn, bias_down])
        if layer == layers - 1:
            mid_own, active[0] = lax.optimization_barrier((mid_own, active[0]))
            parts = row_blocks(matmul_t(jnp.concatenate(active, axis=0), w_down))
            parts = parts[:1] + [part.astype(BF) for part in parts[1:]]
            mid_low = gather_rows(mid_own)
        else:
            shared = [gains[1], shifts[1], gain_two[None], shift_two[None], branches_b[0], branches_b[1]]
            shared = jnp.pad(jnp.concatenate(shared), ((0, 6), (0, 0))).astype(BF)
            blocks = gather_blocks(jnp.concatenate([mid_own, shared], axis=0))
            mid_low = jnp.concatenate([block[:share] for block in blocks], axis=0)
            shared = sum(block[share : share + 10].astype(F32) for block in blocks)
            shared = shared.reshape(10, ranks, share_w)
            shared = lax.dynamic_index_in_dim(shared, rank, 1, False).reshape(-1)
        d_heads = matmul(mid_low, w_out).astype(BF)
        if layer == layers - 1:
            d_heads, parts = lax.optimization_barrier((d_heads, parts))
            state = middle + return_blocks(parts) + branch_bias[layer, 1]
        else:
            d_heads, state_low = lax.optimization_barrier((d_heads, state_low))
            mixed = gather_blocks(state_low)
        d_query, d_own, d_far = attend_backward(half, mask, query, own, far, d_heads, logsum)
        if layer == layers - 1:
            d_query, state_low = lax.optimization_barrier((d_query, state.astype(BF)))
        else:
            d_query, mixed = lax.optimization_barrier((d_query, mixed))
            mixed = restored(mixed, ranks_at, BF)
        d_own = d_own + swap(d_far).astype(F32)
        heads_b[layer] = jnp.stack([jnp.sum(d_query, axis=0), jnp.sum(d_own[1], axis=0)])
        d_projected = jnp.concatenate([d_query, d_own[0], d_own[1]], axis=1).astype(BF)
        if layer == layers - 1:
            d_partial = [matmul_t(block, w_in) for block in row_blocks(d_projected)]
            attn_pairs = [(a_low, d_projected), (mid_low, heads_low)]
        else:
            d_partial = matmul_t(d_projected, w_in)
            line = [jnp.sum(d_partial * first_scaled, axis=0), jnp.sum(d_partial, axis=0), shared]
            line += [heads_b[0].reshape(-1), heads_b[1].reshape(-1), units_b[0], units_b[1]]
            line = jnp.concatenate(line)
            line = jnp.pad(line, (0, shard * 256 - line.shape[0])).astype(BF).reshape(shard, 256)
            line = jnp.broadcast_to(line[None], (size, shard, 256)).reshape(size * shard, 256)
            pairs = [(a_low, d_projected), (mid_low, heads_low)]
            (mine, other), d_partial = lax.optimization_barrier(
                (weight_products(pairs, line, half), d_partial)
            )
            mine = merged(mine, other)
            d_partial = row_blocks(d_partial)
            moved = jnp.sum(exchange(mine, "dp").astype(F32), axis=0)
            last = moved[:, :w4]
            line = moved[:, w4:].reshape(-1)
        if layer == layers - 1:
            parts = return_parts(d_partial)
            grad, own_low, sums = norm_back(parts, a_value, grad_mid, norm_gain[layer, 0])
            gain_one, shift_one = sums[0], sums[1]
        else:
            d_normed = return_blocks(d_partial)
            d_state, gain_one, shift_one = normalize_back(
                d_normed, first_scaled[:share], first_inv[:share], norm_gain[layer, 0]
            )
            own_low = (grad_mid + d_state).astype(BF)
        gains[layer] = jnp.stack([gain_one, gain_two])
        shifts[layer] = jnp.stack([shift_one, shift_two])

    later = reduced(matrices[0])
    all_in, all_out, all_up, all_down = finished(last, early, later, local_w, local_f)

    token_grad = restored(gather_blocks(own_low), ranks_at, F32)
    cut = 2 * width + 10 * share_w
    lines = by_rank(gather_blocks(line[:cut].reshape(-1, share_w)))
    late = jnp.sum(lines[:, : 2 * ranks], axis=0).reshape(2, width)
    shared = lines[:, 2 * ranks :].transpose(1, 0, 2).reshape(10, width)
    gain_grad = jnp.stack([late[0], shared[4], shared[0], shared[1]]).reshape(layers, 2, width)
    shift_grad = jnp.stack([late[1], shared[5], shared[2], shared[3]]).reshape(layers, 2, width)
    branch_grad = shared[6:10].reshape(layers, 2, width)
    head_grad = line[cut : cut + layers * 2 * local_w].reshape(layers, 2, local_w)
    cut += layers * 2 * local_w
    unit_grad = line[cut : cut + layers * local_f].reshape(layers, local_f)
    return (
        mixed.reshape(1, rows, width),
        token_grad.reshape(1, rows, width),
        all_in,
        all_out,
        all_up,
        all_down,
        gain_grad,
        shift_grad,
        head_grad,
        unit_grad,
        branch_grad,
    )


def solution(mesh):
    return jax.shard_map(
        on_device,
        mesh=mesh,
        in_specs=(
            P("dp", "ctx", None),
            P(None, ("dp", "ctx"), None, "mp"),
            P(None, ("dp", "ctx"), "mp"),
            P(None, ("dp", "ctx"), "mp"),
            P(None, ("dp", "ctx"), "mp"),
            P(),
            P(),
            P(None, None, "mp"),
            P(None, "mp"),
            P(),
            P("dp", "ctx", None),
        ),
        out_specs=(
            P("dp", "ctx", None),
            P("dp", "ctx", None),
            P(None, ("dp", "ctx"), None, "mp"),
            P(None, ("dp", "ctx"), "mp"),
            P(None, ("dp", "ctx"), "mp"),
            P(None, ("dp", "ctx"), "mp"),
            P(),
            P(),
            P(None, None, "mp"),
            P(None, "mp"),
            P(),
        ),
        check_vma=False,
    )
```
